32 devices in a mesh: groups: 2 (over x), morton: 16 (over z, y, core).
Axes of the slice: x: 2, y: 2, z: 4, core: 2. Of those that a mesh axis runs over, the one named last changes fastest.
Arguments:
- features: bfloat16 [64, 32, 4096], P(('groups', 'morton')), parts along dimension 0, may hold values from -6 to 6
- voxel_mask: int32 [64, 4096], P(('groups', 'morton')), parts along dimension 0, may hold values 0 or 1
- brick_xy: int32 [64, 2], P('groups'), parts along dimension 0, may hold values from 0 to 3, as said below
- neighbours: int32 [64, 26], P(('groups', 'morton')), parts along dimension 0, may hold values from -1 to 31, as said below
- conv_weight: bfloat16 [32, 864], replicated, may hold values from -0.21875 to 0.21875
- down_weight: bfloat16 [64, 256], replicated, may hold values from -0.375 to 0.375
- coarse_grad: bfloat16 [64, 64, 4096], P(('groups', 'morton')), parts along dimension 0, may hold values from -6 to 6
Outputs:
- coarse_out: bfloat16 [64, 64, 4096], P(('groups', 'morton')), parts along dimension 0
- input_grad: bfloat16 [64, 32, 4096], P(('groups', 'morton')), parts along dimension 0
- conv_grad: float32 [64, 864], P('groups'), parts along dimension 0
- down_grad: float32 [128, 256], P('groups'), parts along dimension 0
The draws below stay inside these ranges and needn't reach their ends.
There are 2 independent parts, one for each index of `groups`. The reference program is written for one: setup_inputs(seed, part) draws one part's arguments, and reference() takes and returns one part's arrays. A program takes and returns all parts, laid end to end along the dimension named above; an argument that names none is the same for every part. Nothing has to cross between parts.
Inputs may be any that keep to these rules, and one draw needn't show every extreme that they name: brick_xy[r] is the (x, y) position of brick r; within a layer no position repeats and the bricks of a layer are in Morton order of (x, y). Brick r lies in z-layer r // 2. neighbours[r, k] is the brick at offset o_k (k < 13) or o_(k+1) (k >= 13) from brick r, with x, y from brick_xy and z the layer, or -1 where that position is empty or outside the 4 x 4 x 32 // 2 grid of positions.
All inputs are finite; a program needn't handle non-finite values. No bound on the sum of `voxel_mask` on one device may be relied on, other than what follows from the above.
Results may differ from the reference program's by a relative error of at most 0.005.
Values may be sent and summed in bfloat16 or wider, within the bound.
No kernel may reach another device: no remote copies, remote signals or barrier semaphores. Data moves between devices by JAX's collectives and lax.ppermute only.
A program may use at most 192 MiB of HBM per device.

```python
import math
import jax
import jax.numpy as jnp
from jax import lax

CH = 32
CH2 = 64
EDGE = 16
SIDE = 4
B = 2
VOX = 4096
BRICKS = 32
COARSE = 32


def alternate(cell_x, cell_y):
    morton_code = jnp.zeros_like(cell_x)
    for bit_index in range(4):
        morton_code = morton_code + cell_x // (1 << bit_index) % 2 * (1 << 2 * bit_index) + cell_y // (1 << bit_index) % 2 * (1 << 2 * bit_index + 1)
    return morton_code


def chosen_cells(key):
    layers = BRICKS // B
    cell_count = SIDE * SIDE
    scores = jax.random.randint(jax.random.fold_in(key, 11), (layers, cell_count), 0, 1 << 20)
    scores = scores * cell_count + jnp.arange(cell_count, dtype=jnp.int32)[None, :]
    picked = jnp.argsort(scores, axis=1, stable=True)[:, :B].astype(jnp.int32)
    morton_code = alternate(picked % SIDE, picked // SIDE)
    ordering = jnp.argsort(morton_code, axis=1, stable=True)
    return jnp.take_along_axis(picked, ordering, axis=1)


def draw_brick_xy(key, part):
    flat_cells = chosen_cells(key).reshape(-1)
    return jnp.stack([flat_cells % SIDE, flat_cells // SIDE], axis=1).astype(jnp.int32)


def draw_neighbours(key, part):
    layers = BRICKS // B
    cell_count = SIDE * SIDE
    picked = chosen_cells(key)
    brick_ids = jnp.arange(BRICKS, dtype=jnp.int32).reshape(layers, B)
    occupancy = jnp.full((layers, cell_count), -1, jnp.int32)
    occupancy = occupancy.at[jnp.arange(layers, dtype=jnp.int32)[:, None], picked].set(brick_ids)
    flat_cells = picked.reshape(-1)
    cell_x = flat_cells % SIDE
    cell_y = flat_cells // SIDE
    layer_of = jnp.arange(BRICKS, dtype=jnp.int32) // B
    columns = []
    for step_z in (-1, 0, 1):
        for step_y in (-1, 0, 1):
            for step_x in (-1, 0, 1):
                if step_x == 0 and step_y == 0 and (step_z == 0):
                    continue
                near_x = cell_x + step_x
                near_y = cell_y + step_y
                near_z = layer_of + step_z
                inside = (near_x >= 0) & (near_x < SIDE) & (near_y >= 0) & (near_y < SIDE) & (near_z >= 0) & (near_z < layers)
                found_id = occupancy[jnp.clip(near_z, 0, layers - 1), jnp.clip(near_y, 0, SIDE - 1) * SIDE + jnp.clip(near_x, 0, SIDE - 1)]
                columns.append(jnp.where(inside, found_id, -1))
    return jnp.stack(columns, axis=1).astype(jnp.int32)


def plant(array, own_key, least, top_value):
    longest = array.shape.index(max(array.shape))
    spots = []
    for shift in (0, 1):
        where = [jax.random.randint(jax.random.fold_in(own_key, axis), (), 0, length) for axis, length in enumerate(array.shape)]
        where[longest] = (where[longest] + shift) % array.shape[longest]
        spots.append(tuple(where))
    return array.at[spots[0]].set(least).at[spots[1]].set(top_value)


def block_levels(key, shape, shards, low, top_value):
    level = 1.0
    for dim, shards_of in shards:
        heights = jax.random.uniform(jax.random.fold_in(jax.random.fold_in(key, 6), dim), (shards_of,), jnp.float32, low / len(shards), top_value / len(shards))
        level = level * jnp.repeat(jnp.exp(heights), shape[dim] // shards_of).reshape((-1,) + (1,) * (len(shape) - 1 - dim))
    return level


def normal_values(own_key, shape, scale, bound, split=(), kind=jnp.bfloat16):
    gain = block_levels(own_key, shape, split, -0.22, 0.18) if split else 1.0
    values = jax.random.normal(own_key, shape, jnp.float32) * scale * gain
    return jnp.minimum(jnp.maximum(values, -bound), bound).astype(kind)


def setup_inputs(seed: int = 0, part: int = 0) -> dict:
    splits = jax.random.split(jax.random.key(seed), 8)
    part_keys = jax.random.split(jax.random.fold_in(splits[7], part), 8)
    features = normal_values(part_keys[0], (BRICKS, CH, VOX), 1.0, 6.0, ((0, 16),))
    voxel_mask = plant((jax.random.randint(part_keys[1], (BRICKS, VOX), 0, 4) < 3).astype(jnp.int32), jax.random.fold_in(part_keys[1], 1), 0, 1)
    brick_xy = draw_brick_xy(jax.random.fold_in(jax.random.fold_in(splits[7], part), 71), part)
    neighbours = draw_neighbours(jax.random.fold_in(jax.random.fold_in(splits[7], part), 71), part)
    conv_weight = normal_values(splits[4], (CH, 27 * CH), (27 * CH) ** -0.5, 0.21875)
    down_weight = normal_values(splits[5], (CH2, 8 * CH), (8 * CH) ** -0.5, 0.375)
    coarse_grad = normal_values(part_keys[6], (COARSE, CH2, VOX), 1.0, 6.0, ((0, 16),))
    return dict(features=features, voxel_mask=voxel_mask, brick_xy=brick_xy, neighbours=neighbours, conv_weight=conv_weight, down_weight=down_weight, coarse_grad=coarse_grad)


OFFSETS = [(step_x, step_y, step_z) for step_z in (-1, 0, 1) for step_y in (-1, 0, 1) for step_x in (-1, 0, 1)]
AROUND = [offset_entry for offset_entry in OFFSETS if offset_entry != (0, 0, 0)]

def source(step, cube_edge):
    if step < 0:
        return slice(cube_edge - 1, cube_edge)
    if step > 0:
        return slice(0, 1)
    return slice(0, cube_edge)

def target(step, cube_edge):
    if step < 0:
        return slice(0, 1)
    if step > 0:
        return slice(cube_edge + 1, cube_edge + 2)
    return slice(1, cube_edge + 1)

def extent(step, cube_edge):
    return cube_edge if step == 0 else 1

def fill_block(center, pieces, cube_edge):
    channels = center.shape[0]
    padded = jnp.zeros((channels, cube_edge + 2, cube_edge + 2, cube_edge + 2), center.dtype)
    padded = padded.at[:, 1:cube_edge + 1, 1:cube_edge + 1, 1:cube_edge + 1].set(center)
    for (step_x, step_y, step_z), piece_data in zip(AROUND, pieces):
        region_shape = (channels, extent(step_z, cube_edge), extent(step_y, cube_edge), extent(step_x, cube_edge))
        padded = padded.at[:, target(step_z, cube_edge), target(step_y, cube_edge), target(step_x, cube_edge)].set(piece_data.reshape(region_shape))
    return padded

def unfold(padded, cube_edge):
    channels = padded.shape[0]
    columns = [padded[:, 1 + step_z:1 + step_z + cube_edge, 1 + step_y:1 + step_y + cube_edge, 1 + step_x:1 + step_x + cube_edge].reshape(channels, cube_edge * cube_edge * cube_edge) for step_x, step_y, step_z in OFFSETS]
    return jnp.concatenate(columns, axis=0)

def split_octants(values, half_edge):
    number, channel_count = (values.shape[0], values.shape[1])
    arranged = values.reshape(number, channel_count, half_edge, 2, half_edge, 2, half_edge, 2)
    arranged = arranged.transpose(0, 3, 5, 7, 1, 2, 4, 6)
    return arranged.reshape(number, 8 * channel_count, half_edge ** 3)

def merge_octants(values, half_edge):
    number = values.shape[0]
    channel_count = values.shape[1] // 8
    arranged = values.reshape(number, 2, 2, 2, channel_count, half_edge, half_edge, half_edge)
    arranged = arranged.transpose(0, 4, 5, 1, 6, 2, 7, 3)
    return arranged.reshape(number, channel_count, 8 * half_edge ** 3)

def join_octants(slots, half_edge):
    number, channel_count = (slots.shape[0], slots.shape[2])
    arranged = slots.reshape(number, 2, 2, 2, channel_count, half_edge, half_edge, half_edge)
    arranged = arranged.transpose(0, 4, 1, 5, 2, 6, 3, 7)
    return arranged.reshape(number, channel_count, 8 * half_edge ** 3)

def part_octants(values, half_edge):
    number, channel_count = (values.shape[0], values.shape[1])
    arranged = values.reshape(number, channel_count, 2, half_edge, 2, half_edge, 2, half_edge)
    arranged = arranged.transpose(0, 2, 4, 6, 1, 3, 5, 7)
    return arranged.reshape(number, 8, channel_count, half_edge ** 3)

def reference(features, voxel_mask, brick_xy, neighbours, conv_weight, down_weight, coarse_grad):
    cube_edge = EDGE
    half_edge = cube_edge // 2
    active_mask = voxel_mask.astype(jnp.bfloat16)
    inputs = features * active_mask[:, None, :]
    brick_rows = jnp.arange(BRICKS, dtype=jnp.int32)

    def padded_of(values, brick_row):
        cubes = values.reshape(values.shape[0], values.shape[1], cube_edge, cube_edge, cube_edge)
        brick_ids = neighbours[brick_row]
        pieces = []
        for column, (step_x, step_y, step_z) in enumerate(AROUND):
            found_id = brick_ids[column]
            cube_data = jnp.take(cubes, jnp.maximum(found_id, 0), axis=0)
            piece_data = cube_data[:, source(step_z, cube_edge), source(step_y, cube_edge), source(step_x, cube_edge)]
            pieces.append(jnp.where(found_id >= 0, piece_data, jnp.zeros_like(piece_data)))
        return fill_block(cubes[brick_row], pieces, cube_edge)

    def forward_one(brick_row):
        return jnp.dot(conv_weight, unfold(padded_of(inputs, brick_row), cube_edge), preferred_element_type=jnp.float32)
    before = lax.map(forward_one, brick_rows)
    active = (jax.nn.silu(before) * active_mask[:, None, :]).astype(jnp.bfloat16)
    stride_cols = split_octants(active, half_edge)
    octants = jnp.einsum('oc,rcw->row', down_weight.astype(jnp.float32), stride_cols.astype(jnp.float32), precision=lax.Precision.HIGHEST).astype(jnp.bfloat16)
    layer_of = brick_rows // B
    cell_x = brick_xy[:, 0]
    cell_y = brick_xy[:, 1]
    coarse_id = 4 * (layer_of // 2) + 2 * (cell_y // 2) + cell_x // 2
    slot_index = 4 * (layer_of % 2) + 2 * (cell_y % 2) + cell_x % 2
    slots = jnp.zeros((COARSE, 8, CH2, half_edge ** 3), jnp.bfloat16).at[coarse_id, slot_index].set(octants)
    coarse_out = join_octants(slots, half_edge)
    grad_slots = part_octants(coarse_grad, half_edge)
    grad_oct = grad_slots[coarse_id, slot_index]
    down_sum = jnp.einsum('row,rcw->oc', grad_oct.astype(jnp.float32), stride_cols.astype(jnp.float32), precision=lax.Precision.HIGHEST)
    grad_cols = jnp.einsum('oc,row->rcw', down_weight.astype(jnp.float32), grad_oct.astype(jnp.float32), precision=lax.Precision.HIGHEST)
    grad_act = merge_octants(grad_cols, half_edge)
    sigmoid_part = jax.nn.sigmoid(before)
    grad_pre = (grad_act * active_mask[:, None, :] * sigmoid_part * (1.0 + before * (1.0 - sigmoid_part))).astype(jnp.bfloat16)
    flipped = conv_weight.reshape(CH, 27, CH)[:, ::-1, :].transpose(2, 1, 0).reshape(CH, 27 * CH)

    def backward_one(running, brick_row):
        columns_g = unfold(padded_of(grad_pre, brick_row), cube_edge)
        columns_x = unfold(padded_of(inputs, brick_row), cube_edge)
        grad_in = jnp.dot(flipped, columns_g, preferred_element_type=jnp.float32)
        running = running + lax.dot_general(grad_pre[brick_row], columns_x, (((1,), (1,)), ((), ())), preferred_element_type=jnp.float32)
        return (running, grad_in)
    conv_sum, grad_x = lax.scan(backward_one, jnp.zeros((CH, 27 * CH), jnp.float32), brick_rows)
    input_grad = (grad_x * active_mask[:, None, :]).astype(jnp.bfloat16)
    grad_scale = 1.0 / math.sqrt(BRICKS * VOX)
    return (coarse_out, input_grad, conv_sum * grad_scale, down_sum * grad_scale)
```

```python
import functools
import math

import jax
import jax.numpy as jnp
from jax import lax
from jax.experimental import pallas as pl
from jax.experimental.pallas import tpu as pltpu
from jax.sharding import PartitionSpec as P

EDGE = 16
HALF = 8
PLANE = EDGE * EDGE
QUARTER = HALF * HALF
BF16 = jnp.bfloat16
F32 = jnp.float32
I32 = jnp.int32
VMEM_LIMIT = 48 * 1024 * 1024


def iota(shape, dim):
    return lax.broadcasted_iota(I32, shape, dim)


def one_hot(row_key, column_key):
    return jnp.where(row_key == column_key, 1.0, 0.0).astype(BF16)


def mm(a, b):
    return jnp.dot(a, b, preferred_element_type=F32)


def mm_nt(a, b):
    return lax.dot_general(a, b, (((1,), (1,)), ((), ())), preferred_element_type=F32)


def xy_of(xy_ref, layer, brick):
    return xy_ref[layer * 2 + brick, 0], xy_ref[layer * 2 + brick, 1]


def octant_key(xy_ref, layer, parity, lane):
    brick = (lane >> 6) & 1
    bases = []
    for b in range(2):
        x, y = xy_of(xy_ref, layer, b)
        base = (x // 2) * PLANE + (y % 2) * HALF * EDGE + (x % 2) * HALF
        bases.append(jnp.where(y // 2 == parity, base, -65536))
    return jnp.where(brick == 0, bases[0], bases[1]) + ((lane >> 3) & 7) * EDGE + (lane & 7)


def first_kernel(layers, xy_ref, grad_ref, feat_ref, mask_ref, low_ref, high_ref, own_ref, send_ref):
    layer = lax.axis_index("morton")
    parity = layer % 2
    for r in range(2):
        for z, ref in ((0, low_ref), (EDGE - 1, high_ref)):
            lanes = pl.ds(z * PLANE, PLANE)
            mask = mask_ref[pl.ds(r, 1), lanes].astype(F32).astype(BF16)
            ref[:, pl.ds(r * PLANE, PLANE)] = feat_ref[r, :, lanes] * mask
    partner = layer + 1 - 2 * parity
    for target, half, ref in ((partner, 1 - parity, send_ref), (layer, parity, own_ref)):
        row = iota((2 * PLANE, 2 * QUARTER), 0)
        lane = iota((2 * PLANE, 2 * QUARTER), 1)
        pick = one_hot(row, octant_key(xy_ref, target, parity, lane))
        for wz in range(HALF):
            lanes = pl.ds(pl.multiple_of((half * HALF + wz) * PLANE, PLANE), PLANE)
            planes = jnp.concatenate([grad_ref[0, :, lanes], grad_ref[1, :, lanes]], axis=1)
            ref[:, pl.ds(wz * 2 * QUARTER, 2 * QUARTER)] = mm(planes, pick).astype(BF16)


def build_selection(xy_ref, layer, other, r, sel_ref):
    x, y = xy_of(xy_ref, layer, r)
    row = iota((2 * PLANE, 128), 0)
    bases = []
    for s in range(2):
        near_x, near_y = xy_of(xy_ref, other, s)
        bases.append((near_y - y) * EDGE * 1024 + (near_x - x) * EDGE)
    row_key = jnp.where(row < PLANE, bases[0], bases[1]) + ((row >> 4) & 15) * 1024 + (row & 15)
    for tile in range(9):
        lane = iota((2 * PLANE, 128), 1) + (tile % 3) * 128
        key = ((lane >> 4) - 1) * 1024 + (lane & 15) + (tile // 3 - 1)
        if tile % 3 == 2:
            key = jnp.where(lane < 18 * EDGE, key, -(1 << 24))
        sel_ref[:, pl.ds(tile * 128, 128)] = one_hot(row_key, key)


def unfold_rows(source, sel_ref, r, first_plane, cols_ref):
    planes = source.shape[0] // 32
    for dx in range(3):
        wide = mm(source, sel_ref[:, dx * 384 : (dx + 1) * 384]).astype(BF16)
        for dy in range(3):
            piece = wide[:, EDGE * dy : EDGE * dy + PLANE]
            for p in range(planes):
                start = (first_plane + p) * 288 + (dy * 3 + dx) * 32
                cols_ref[r, pl.ds(start, 32), :] = piece[p * 32 : (p + 1) * 32]


def unfold_all(xy_ref, layers, own_rows, low, high, sel_ref, cols_ref):
    layer = lax.axis_index("morton")
    for r in range(2):
        build_selection(xy_ref, layer, layer, r, sel_ref)
        for p in range(0, EDGE, 4):
            unfold_rows(own_rows(p, 4), sel_ref, r, 1 + p, cols_ref)
        build_selection(xy_ref, layer, jnp.maximum(layer - 1, 0), r, sel_ref)
        unfold_rows(low, sel_ref, r, 0, cols_ref)
        build_selection(xy_ref, layer, jnp.minimum(layer + 1, layers - 1), r, sel_ref)
        unfold_rows(high, sel_ref, r, EDGE + 1, cols_ref)


def convolve(weight, cols_ref, acc_ref):
    stacked = jnp.concatenate([weight[:, dz * 288 : (dz + 1) * 288] for dz in range(3)], axis=0)
    for r in range(2):
        acc_ref[r] = jnp.zeros(acc_ref.shape[1:], F32)
        for p in range(EDGE + 2):
            rows = pl.ds((EDGE + 1 - p) * 32, 96)
            acc_ref[r, rows, :] += mm(stacked, cols_ref[r, pl.ds(p * 288, 288), :])


def second_kernel(
    layers, scale, xy_ref, feat_ref, mask_ref, low_ref, high_ref, own_ref, recv_ref, weight_ref, down_ref, down_t_ref,
    oct_ref, gplanes_ref, glow_ref, ghigh_ref, sums_ref,
    in_ref, sel_ref, cols_ref, acc_ref, act_ref, up_ref, stride_ref, grad_ref,
):
    for r in range(2):
        for z in range(EDGE):
            lanes = pl.ds(z * PLANE, PLANE)
            mask = mask_ref[pl.ds(r, 1), lanes].astype(F32).astype(BF16)
            in_ref[pl.ds(z * 32, 32), pl.ds(r * PLANE, PLANE)] = feat_ref[r, :, lanes] * mask
    unfold_all(
        xy_ref, layers, lambda p, n: in_ref[pl.ds(p * 32, n * 32), :], low_ref[...], high_ref[...], sel_ref, cols_ref
    )
    convolve(weight_ref[...], cols_ref, acc_ref)

    grad_oct = own_ref[...] + recv_ref[...]
    pieces = jnp.concatenate([grad_oct[:, wz * 128 : (wz + 1) * 128] for wz in range(HALF)], axis=0)
    row = iota((128, PLANE), 0)
    lane = iota((128, PLANE), 1)
    for r in range(2):
        row_key = jnp.where((row >> 6) == r, ((row >> 3) & 7) * 128 + (row & 7) * 2, -65536)
        for k in range(4):
            key = ((lane >> 4) - k // 2) * 64 + (lane & 15) - k % 2
            spread = mm(pieces, one_hot(row_key, key)).astype(BF16)
            for wz in range(HALF):
                up_ref[r, wz, pl.ds(k * 64, 64), :] = spread[wz * 64 : (wz + 1) * 64]
    zeros = jnp.zeros((64, PLANE), BF16)
    for r in range(2):
        grad_ref[r, pl.ds(0, 64), :] = zeros
        grad_ref[r, pl.ds(18 * 32, 64), :] = zeros
        for wz in range(HALF):
            grad_act = mm(down_t_ref[...], up_ref[r, wz])
            for kz in range(2):
                z = 2 * wz + kz
                mask = mask_ref[pl.ds(r, 1), pl.ds(z * PLANE, PLANE)].astype(F32)
                pre = acc_ref[r, pl.ds((17 - z) * 32, 32), :]
                sig = 1.0 / (1.0 + jnp.exp(-pre))
                masked = sig * mask
                act_ref[pl.ds(z * 32, 32), pl.ds(r * PLANE, PLANE)] = (pre * masked).astype(BF16)
                grad = grad_act[kz * 32 : (kz + 1) * 32] * masked * (1.0 + pre * (1.0 - sig))
                grad = grad.astype(BF16)
                grad_ref[r, pl.ds((17 - z) * 32, 32), :] = grad
                gplanes_ref[pl.ds(z * 32, 32), pl.ds(r * PLANE, PLANE)] = grad
                if z == 0:
                    glow_ref[:, pl.ds(r * PLANE, PLANE)] = grad
                if z == EDGE - 1:
                    ghigh_ref[:, pl.ds(r * PLANE, PLANE)] = grad

    row = iota((2 * PLANE, 128), 0)
    lane = iota((2 * PLANE, 128), 1)
    row_key = (row >> 8) * 4096 + ((row >> 4) & 15) * 64 + (row & 15)
    lane_key = (lane >> 6) * 4096 + ((lane >> 3) & 7) * 128 + (lane & 7) * 2
    for k in range(4):
        gather = one_hot(row_key, lane_key + (k // 2) * 64 + k % 2)
        found = mm(act_ref[...], gather).astype(BF16)
        for z in range(EDGE):
            rows = pl.ds((z % 2) * 128 + k * 32, 32)
            stride_ref[rows, pl.ds((z // 2) * 128, 128)] = found[z * 32 : (z + 1) * 32]
    oct_ref[...] = mm(down_ref[...], stride_ref[...]).astype(BF16)
    down_sum = mm_nt(grad_oct, stride_ref[...]) * scale
    sums_ref[:, pl.ds(896, 256)] = down_sum[:32]
    sums_ref[:, pl.ds(1152, 256)] = down_sum[32:]

    total = jnp.zeros((96, 288), F32)
    for r in range(2):
        for p in range(EDGE + 2):
            total += mm_nt(grad_ref[r, pl.ds((EDGE + 1 - p) * 32, 96), :], cols_ref[r, pl.ds(p * 288, 288), :])
    total = total * scale
    sums_ref[:, pl.ds(0, 896)] = jnp.concatenate(
        [total[:32], total[32:64], total[64:], jnp.zeros((32, 32), F32)], axis=1
    )


def third_kernel(
    layers, xy_ref, gplanes_ref, low_ref, high_ref, mask_ref, flipped_ref, out_ref, sel_ref, cols_ref, acc_ref
):
    unfold_all(
        xy_ref, layers, lambda p, n: gplanes_ref[pl.ds(p * 32, n * 32), :], low_ref[...], high_ref[...], sel_ref, cols_ref
    )
    convolve(flipped_ref[...], cols_ref, acc_ref)
    for r in range(2):
        for z in range(EDGE):
            lanes = pl.ds(z * PLANE, PLANE)
            mask = mask_ref[pl.ds(r, 1), lanes].astype(F32)
            out_ref[r, :, lanes] = (acc_ref[r, pl.ds((17 - z) * 32, 32), :] * mask).astype(BF16)


def coarse_kernel(layers, xy_ref, own_ref, recv_ref, out_ref):
    layer = lax.axis_index("morton")
    parity = layer % 2
    partner = layer + 1 - 2 * parity
    for target, half, ref in ((layer, parity, own_ref), (partner, 1 - parity, recv_ref)):
        pieces = jnp.concatenate([ref[:, wz * 128 : (wz + 1) * 128] for wz in range(HALF)], axis=0)
        key = octant_key(xy_ref, target, parity, iota((128, PLANE), 0))
        for q in range(2):
            lane = iota((128, PLANE), 1) + q * PLANE
            placed = mm(pieces, one_hot(key, lane)).astype(BF16)
            for wz in range(HALF):
                lanes = pl.ds(pl.multiple_of((half * HALF + wz) * PLANE, PLANE), PLANE)
                out_ref[q, :, lanes] = placed[wz * 64 : (wz + 1) * 64]


def call(body, name, out_shapes, operands, scratch=(), flops=0, moved=0):
    specs = [pl.BlockSpec(memory_space=pltpu.SMEM)]
    specs += [pl.BlockSpec(memory_space=pltpu.VMEM)] * (len(operands) - 1)
    return pl.pallas_call(
        body,
        name=name,
        out_shape=out_shapes,
        in_specs=specs,
        out_specs=jax.tree.map(lambda _: pl.BlockSpec(memory_space=pltpu.VMEM), out_shapes),
        scratch_shapes=list(scratch),
        compiler_params=pltpu.CompilerParams(vmem_limit_bytes=VMEM_LIMIT),
        cost_estimate=pl.CostEstimate(flops=flops, bytes_accessed=moved, transcendentals=0),
    )(*operands)


def shape(dims, dtype=BF16):
    return jax.ShapeDtypeStruct(dims, dtype)


def exchange(value, bit):
    return lax.ppermute(value, "morton", [(i, i ^ (1 << bit)) for i in range(lax.axis_size("morton"))])


def sum_over_layers(part):
    layers = lax.axis_size("morton")
    rounds = layers.bit_length() - 1
    odd = lax.axis_index("morton") % 2
    rows = part.shape[0] // 2
    keep = lax.dynamic_slice_in_dim(part, odd * rows, rows, 0)
    away = lax.dynamic_slice_in_dim(part, (1 - odd) * rows, rows, 0)
    total = keep + exchange(away, 0)
    for bit in range(1, rounds):
        total = total + exchange(total, bit)
    other = exchange(total, 0)
    return jnp.where(odd == 0, jnp.concatenate([total, other]), jnp.concatenate([other, total]))


def with_both_sides(low_plane, high_plane):
    layers = lax.axis_size("morton")
    up = [(i, i + 1) for i in range(layers - 1)]
    down = [(i + 1, i) for i in range(layers - 1)]
    return lax.ppermute(high_plane, "morton", up), lax.ppermute(low_plane, "morton", down)


def per_device(features, voxel_mask, brick_xy, neighbours, conv_weight, down_weight, coarse_grad):
    bricks, channels, voxels = features.shape
    layers = lax.axis_size("morton")
    scale = 1.0 / math.sqrt(bricks * layers * voxels)
    side_shape = shape((32, 2 * PLANE))
    oct_shape = shape((64, 1024))
    low, high, own, away = call(
        functools.partial(first_kernel, layers), "select", [side_shape, side_shape, oct_shape, oct_shape],
        (brick_xy, coarse_grad, features, voxel_mask), flops=2 * 2**27, moved=2 << 20,
    )
    from_below, from_above = with_both_sides(low, high)
    arrived = exchange(away, 0)
    down_t = down_weight.reshape(64, 2, 4, 32).transpose(1, 3, 2, 0).reshape(64, 256)
    flipped = conv_weight.reshape(32, 27, 32)[:, ::-1, :].transpose(2, 1, 0).reshape(32, 864)
    cols = pltpu.VMEM((2, 18 * 288, PLANE), BF16)
    acc = pltpu.VMEM((2, 20 * 32, PLANE), F32)
    sel = pltpu.VMEM((2 * PLANE, 1152), BF16)
    octants, gplanes, glow, ghigh, sums = call(
        functools.partial(second_kernel, layers, scale), "forward",
        [oct_shape, shape((512, 512)), side_shape, side_shape, shape((32, 1408), F32)],
        (brick_xy, features, voxel_mask, from_below, from_above, own, arrived, conv_weight, down_weight, down_t),
        scratch=[
            pltpu.VMEM((512, 512), BF16), sel, cols, acc, pltpu.VMEM((512, 512), BF16),
            pltpu.VMEM((2, HALF, 256, PLANE), BF16), pltpu.VMEM((256, 1024), BF16), pltpu.VMEM((2, 20 * 32, PLANE), BF16),
        ],
        flops=6 * 2**30, moved=3 << 20,
    )
    grad_below, grad_above = with_both_sides(glow, ghigh)
    octants_there = exchange(octants, 0)
    total = sum_over_layers(sums)
    input_grad = call(
        functools.partial(third_kernel, layers), "backward", shape((bricks, channels, voxels)),
        (brick_xy, gplanes, grad_below, grad_above, voxel_mask, flipped), scratch=[sel, cols, acc],
        flops=3 * 2**30, moved=1 << 20,
    )
    coarse_out = call(
        functools.partial(coarse_kernel, layers), "place", shape((2, 64, voxels)),
        (brick_xy, octants, octants_there), flops=2**28, moved=1 << 20,
    )
    conv_grad = total[:, :864]
    down_grad = jnp.concatenate([total[:, 896:1152], total[:, 1152:]], axis=0)
    return coarse_out, input_grad, conv_grad, down_grad


def solution(mesh):
    return jax.shard_map(
        per_device,
        mesh=mesh,
        in_specs=(
            P(("groups", "morton"), None, None),
            P(("groups", "morton"), None),
            P("groups", None),
            P(("groups", "morton"), None),
            P(),
            P(),
            P(("groups", "morton"), None, None),
        ),
        out_specs=(
            P(("groups", "morton"), None, None),
            P(("groups", "morton"), None, None),
            P("groups", None),
            P("groups", None),
        ),
        check_vma=False,
    )
```

```python
import functools
import math

import jax
import jax.numpy as jnp
from jax import lax
from jax.experimental import pallas as pl
from jax.experimental.pallas import tpu as pltpu
from jax.sharding import PartitionSpec as P

EDGE = 16
HALF = 8
PLANE = EDGE * EDGE
QUARTER = HALF * HALF
BF16 = jnp.bfloat16
F32 = jnp.float32
I32 = jnp.int32
STEP = 8


def iota(shape, dim):
    return lax.broadcasted_iota(I32, shape, dim)


def one_hot(row_key, column_key):
    return jnp.where(row_key == column_key, 1.0, 0.0).astype(BF16)


def mm(a, b):
    return jnp.dot(a, b, preferred_element_type=F32)


def mm_nt(a, b):
    return lax.dot_general(a, b, (((1,), (1,)), ((), ())), preferred_element_type=F32)


def xy_of(xy_ref, layer, brick):
    return xy_ref[0, layer * 2 + brick], xy_ref[1, layer * 2 + brick]


def octant_key(xy_ref, layer, parity, lane):
    brick = (lane >> 6) & 1
    bases = []
    for b in range(2):
        x, y = xy_of(xy_ref, layer, b)
        base = (x // 2) * PLANE + (y % 2) * HALF * EDGE + (x % 2) * HALF
        bases.append(jnp.where(y // 2 == parity, base, -65536))
    return jnp.where(brick == 0, bases[0], bases[1]) + ((lane >> 3) & 7) * EDGE + (lane & 7)


def start_all(pairs, sems):
    copies = [pltpu.make_async_copy(source, target, sems.at[i]) for i, (source, target) in enumerate(pairs)]
    for copy in copies:
        copy.start()
    return copies


def prepare_kernel(
    xy_ref, feat_hbm, mask_hbm, grad_hbm, weight_hbm, down_hbm,
    core_ref, cross_ref, own_ref, send_ref, flipped_ref, stacked_ref, down_t_ref,
    feat_ref, mask_ref, grad_ref, weight_ref, down_ref, sems,
):
    layer = lax.axis_index("morton")
    parity = layer % 2
    partner = layer + 1 - 2 * parity
    halves = [
        grad_hbm.at[:, :, pl.ds(pl.multiple_of(half * HALF * PLANE, HALF * PLANE), HALF * PLANE)]
        for half in (1 - parity, parity)
    ]
    copies = start_all(
        ((halves[0], grad_ref.at[0]), (halves[1], grad_ref.at[1]), (weight_hbm, weight_ref), (down_hbm, down_ref)), sems
    )
    edges = []
    for side in range(2):
        z = jnp.where(parity == side, EDGE - 1, 0)
        lanes = pl.ds(pl.multiple_of(z * PLANE, PLANE), PLANE)
        edges += start_all(
            ((feat_hbm.at[:, :, lanes], feat_ref.at[side]), (mask_hbm.at[:, lanes], mask_ref.at[side])),
            sems.at[pl.ds(4 + 2 * side, 2)],
        )
    row = iota((2 * PLANE, 2 * QUARTER), 0)
    lane = iota((2 * PLANE, 2 * QUARTER), 1)
    picks = [one_hot(row, octant_key(xy_ref, target, parity, lane)) for target in (partner, layer)]
    for copy in edges:
        copy.wait()
    for side, ref in enumerate((core_ref, cross_ref)):
        for r in range(2):
            mask = mask_ref[side, pl.ds(r, 1), :].astype(F32).astype(BF16)
            ref[:, pl.ds(r * PLANE, PLANE)] = feat_ref[side, r] * mask
    for i, ref in enumerate((send_ref, own_ref)):
        copies[i].wait()
        for wz in range(HALF):
            lanes = pl.ds(wz * PLANE, PLANE)
            planes = jnp.concatenate([grad_ref[i, 0, :, lanes], grad_ref[i, 1, :, lanes]], axis=1)
            ref[:, pl.ds(wz * 2 * QUARTER, 2 * QUARTER)] = mm(planes, picks[i]).astype(BF16)
    copies[2].wait()
    copies[3].wait()
    turned = weight_ref[...].astype(F32).T.astype(BF16)
    for dz in range(3):
        rows = pl.ds(dz * 32, 32)
        blocks = [turned[j * 32 : (j + 1) * 32] for j in (26 - dz * 9 - s for s in range(9))]
        flipped_ref[rows, :] = jnp.concatenate(blocks, axis=1)
        stacked_ref[rows, :] = weight_ref[:, pl.ds(dz * 288, 288)]
    turned = down_ref[...].astype(F32).T.astype(BF16)
    for kz in range(2):
        blocks = [turned[(kz * 4 + k) * 32 : (kz * 4 + k + 1) * 32] for k in range(4)]
        down_t_ref[pl.ds(kz * 32, 32), :] = jnp.concatenate(blocks, axis=1)


def window_mask(shift, ox, oy):
    dy, dx = shift // 3 - 1, shift % 3 - 1
    voxel = (iota((1, PLANE), 1) - (EDGE * dy + dx)) & (PLANE - 1)
    x = (voxel & (EDGE - 1)) + dx - EDGE * ox
    y = (voxel >> 4) + dy - EDGE * oy
    inside = jnp.where(((x | y) & -EDGE) == 0, 1.0, 0.0)
    return jnp.broadcast_to(inside, (32, PLANE)).astype(BF16)


def offset_of(xy_ref, layer, r, other, s):
    x, y = xy_of(xy_ref, layer, r)
    near_x, near_y = xy_of(xy_ref, other, s)
    return near_x - x, near_y - y


def turned(planes, ox):
    return pltpu.roll(planes, (ox * EDGE) & (PLANE - 1), 1)


def shifted(first, second, masks, shift):
    dy, dx = shift // 3 - 1, shift % 3 - 1
    times = first.shape[0] // 32
    both = first * jnp.tile(masks[0], (times, 1)) + second * jnp.tile(masks[1], (times, 1))
    back = (-(EDGE * dy + dx)) & (PLANE - 1)
    return pltpu.roll(both, back, 1) if back else both


def build_masks(xy_ref, layer, r, mask_ref):
    ox, oy = offset_of(xy_ref, layer, r, layer, 1 - r)
    for shift in range(9):
        mask_ref[0, shift] = window_mask(shift, 0, 0)
        mask_ref[1, shift] = window_mask(shift, ox, oy)
    return ox


def unfold_planes(planes_ref, r, ox, mask_ref, cols_ref):
    for p in range(0, EDGE, STEP):
        rows = pl.ds(p * 32, STEP * 32)
        own = planes_ref[rows, pl.ds(r * PLANE, PLANE)]
        other = turned(planes_ref[rows, pl.ds((1 - r) * PLANE, PLANE)], ox)
        for shift in range(9):
            piece = own if shift == 4 else shifted(own, other, (mask_ref[0, shift], mask_ref[1, shift]), shift)
            for q in range(STEP):
                cols_ref[pl.ds((p + q) * 288 + shift * 32, 32), :] = piece[q * 32 : (q + 1) * 32]


def unfold_side(xy_ref, layer, r, other, planes):
    places = [offset_of(xy_ref, layer, r, other, s) for s in range(2)]
    first, second = (turned(planes[:, s * PLANE : (s + 1) * PLANE], places[s][0]) for s in range(2))
    pieces = []
    for shift in range(9):
        masks = [window_mask(shift, ox, oy) for ox, oy in places]
        pieces.append(shifted(first, second, masks, shift))
    return jnp.concatenate(pieces, axis=0)


def convolve(stacked, cols_ref, acc_ref):
    acc_ref[...] = jnp.zeros(acc_ref.shape, F32)
    for p in range(EDGE):
        rows = pl.ds((EDGE - p) * 32, 96)
        acc_ref[rows, :] += mm(stacked, cols_ref[pl.ds(p * 288, 288), :])


def inner_kernel(
    xy_ref, feat_hbm, mask_hbm, stacked_hbm, cols_hbm, acc_hbm,
    feat_ref, mask_ref, stacked_ref, window_ref, in_ref, cols_ref, acc_ref, sems,
):
    layer = lax.axis_index("morton")
    copies = start_all(((feat_hbm, feat_ref), (mask_hbm, mask_ref), (stacked_hbm, stacked_ref)), sems)
    ox = [build_masks(xy_ref, layer, r, window_ref.at[r]) for r in range(2)]
    for copy in copies:
        copy.wait()
    for r in range(2):
        for z in range(EDGE):
            lanes = pl.ds(z * PLANE, PLANE)
            mask = mask_ref[pl.ds(r, 1), lanes].astype(F32).astype(BF16)
            in_ref[pl.ds(z * 32, 32), pl.ds(r * PLANE, PLANE)] = feat_ref[r, :, lanes] * mask
    out = []
    for r in range(2):
        unfold_planes(in_ref, r, ox[r], window_ref.at[r], cols_ref.at[r])
        convolve(stacked_ref[...], cols_ref.at[r], acc_ref.at[r])
        out += start_all(
            ((cols_ref.at[r], cols_hbm.at[r]), (acc_ref.at[r, pl.ds(64, 512)], acc_hbm.at[r, pl.ds(0, 512)])), sems.at[pl.ds(3 + 2 * r, 2)]
        )
    for copy in out:
        copy.wait()


def sides_of(layer, layers):
    odd = layer % 2
    above = layer + 1 - odd
    core = jnp.where(odd == 0, layer + 1, layer - 1)
    cross = jnp.where(odd == 0, jnp.maximum(layer - 1, 0), jnp.minimum(layer + 1, layers - 1))
    return ((core, 2 * (1 - odd), 15 * (1 - odd)), (cross, 2 * odd, 15 * odd))


def rows_at(index):
    return pl.ds(pl.multiple_of(index * 32, 32), 32)


def outer_kernel(
    layers, scale, xy_ref, cols_hbm, acc_hbm, mask_hbm, down_hbm, core_ref, cross_ref, own_ref, recv_ref, stacked_ref, down_t_ref,
    oct_ref, gplanes_ref, gcore_ref, gcross_ref, sums_ref,
    cols_ref, acc_ref, mask_ref, down_ref, act_ref, up_ref, stride_ref, grad_ref, total_ref, sems,
):
    copies = start_all(
        ((acc_hbm.at[:, pl.ds(0, 512)], acc_ref), (mask_hbm, mask_ref), (down_hbm, down_ref), (cols_hbm, cols_ref)), sems
    )
    layer = lax.axis_index("morton")
    sides = sides_of(layer, layers)

    grad_oct = own_ref[...] + recv_ref[...]
    pieces = jnp.concatenate([grad_oct[:, wz * 128 : (wz + 1) * 128] for wz in range(HALF)], axis=0)
    row = iota((128, PLANE), 0)
    lane = iota((128, PLANE), 1)
    parities = []
    for k in range(4):
        voxel = iota((1, PLANE), 1)
        hit = jnp.where(((voxel >> 4) & 1) * 2 + (voxel & 1) == k, 1.0, 0.0)
        parities.append(jnp.broadcast_to(hit, (64, PLANE)).astype(BF16))
    for r in range(2):
        row_key = jnp.where((row >> 6) == r, row & 63, -1)
        spread = mm(pieces, one_hot(row_key, (lane >> 5) * HALF + ((lane >> 1) & 7))).astype(BF16)
        for wz in range(HALF):
            for k in range(4):
                up_ref[r, wz, pl.ds(k * 64, 64), :] = spread[wz * 64 : (wz + 1) * 64] * parities[k]
    side_cols = []
    for (other, dz, z), ref in zip(sides, (core_ref, cross_ref)):
        for r in range(2):
            side_cols.append(unfold_side(xy_ref, layer, r, other, ref[...]))
    for copy in copies[:3]:
        copy.wait()
    for side, (other, dz, z) in enumerate(sides):
        for r in range(2):
            acc_ref[r, rows_at(15 - z), :] += mm(stacked_ref[rows_at(dz), :], side_cols[side * 2 + r])
    zeros = jnp.zeros((64, PLANE), BF16)
    for r in range(2):
        grad_ref[r, pl.ds(0, 64), :] = zeros
        grad_ref[r, pl.ds(18 * 32, 64), :] = zeros
        for wz in range(HALF):
            grad_act = mm(down_t_ref[...], up_ref[r, wz])
            for kz in range(2):
                z = 2 * wz + kz
                mask = mask_ref[pl.ds(r, 1), pl.ds(z * PLANE, PLANE)].astype(F32)
                pre = acc_ref[r, pl.ds((15 - z) * 32, 32), :]
                sig = 1.0 / (1.0 + jnp.exp(-pre))
                masked = sig * mask
                act_ref[pl.ds(z * 32, 32), pl.ds(r * PLANE, PLANE)] = (pre * masked).astype(BF16)
                grad = grad_act[kz * 32 : (kz + 1) * 32] * masked * (1.0 + pre * (1.0 - sig))
                grad = grad.astype(BF16)
                grad_ref[r, pl.ds((17 - z) * 32, 32), :] = grad
                gplanes_ref[pl.ds(z * 32, 32), pl.ds(r * PLANE, PLANE)] = grad
        for (other, dz, z), ref in zip(sides, (gcore_ref, gcross_ref)):
            ref[:, pl.ds(r * PLANE, PLANE)] = grad_ref[r, rows_at(17 - z), :]

    row = iota((2 * PLANE, PLANE), 0)
    lane = iota((2 * PLANE, PLANE), 1)
    row_key = (row >> 8) * 4096 + ((row >> 4) & 15) * 64 + (row & 15)
    lane_key = ((lane >> 6) & 1) * 4096 + ((lane >> 3) & 7) * 128 + (lane & 7) * 2 + (lane >> 7)
    for ky in range(2):
        found = mm(act_ref[...], one_hot(row_key, lane_key + ky * 64)).astype(BF16)
        for z in range(EDGE):
            for kx in range(2):
                rows = pl.ds((z % 2) * 128 + (ky * 2 + kx) * 32, 32)
                stride_ref[rows, pl.ds((z // 2) * 128, 128)] = found[z * 32 : (z + 1) * 32, kx * 128 : (kx + 1) * 128]
    oct_ref[...] = mm(down_ref[...], stride_ref[...]).astype(BF16)
    down_sum = mm_nt(grad_oct, stride_ref[...]) * scale
    sums_ref[:, pl.ds(896, 256)] = down_sum[:32]
    sums_ref[:, pl.ds(1152, 256)] = down_sum[32:]

    copies[3].wait()
    total = jnp.zeros((288, 96), F32)
    for r in range(2):
        for p in range(EDGE):
            total += mm_nt(cols_ref[r, pl.ds(p * 288, 288), :], grad_ref[r, pl.ds((EDGE - p) * 32, 96), :])
    total_ref[...] = total.T
    for side, (other, dz, z) in enumerate(sides):
        for r in range(2):
            total_ref[rows_at(dz), :] += mm_nt(grad_ref[r, rows_at(17 - z), :], side_cols[side * 2 + r])
    total = [total_ref[pl.ds(dz * 32, 32), :] for dz in range(3)]
    sums_ref[:, pl.ds(0, 896)] = jnp.concatenate([*total, jnp.zeros((32, 32), F32)], axis=1) * scale


def back_inner_kernel(r, xy_ref, after_ref, gplanes_ref, flipped_ref, acc_ref, window_ref, cols_ref):
    layer = lax.axis_index("morton")
    ox = build_masks(xy_ref, layer, r, window_ref)
    unfold_planes(gplanes_ref, r, ox, window_ref, cols_ref)
    convolve(flipped_ref[...], cols_ref, acc_ref)


def back_outer_kernel(
    layers, xy_ref, mask_hbm, after_ref, acc0_ref, acc1_ref, core_ref, cross_ref, flipped_ref, out_ref,
    mask_ref, sums_ref, sems,
):
    copies = start_all(((mask_hbm, mask_ref),), sems)
    layer = lax.axis_index("morton")
    sides = sides_of(layer, layers)
    for r, acc_ref in enumerate((acc0_ref, acc1_ref)):
        sums_ref[r] = acc_ref[pl.ds(64, 512), :]
        for (other, dz, z), ref in zip(sides, (core_ref, cross_ref)):
            cols = unfold_side(xy_ref, layer, r, other, ref[...])
            sums_ref[r, rows_at(15 - z), :] += mm(flipped_ref[rows_at(dz), :], cols)
    copies[0].wait()
    for r in range(2):
        for z in range(EDGE):
            lanes = pl.ds(z * PLANE, PLANE)
            mask = mask_ref[pl.ds(r, 1), lanes].astype(F32)
            out_ref[r, :, lanes] = (sums_ref[r, pl.ds((15 - z) * 32, 32), :] * mask).astype(BF16)


def finish_kernel(total_ref, other_ref, conv_ref, down_ref):
    odd = lax.axis_index("morton") % 2
    for place, ref in ((odd, total_ref), (1 - odd, other_ref)):
        rows = pl.ds(pl.multiple_of(place * 16, 16), 16)
        conv_ref[rows, :] = ref[:, pl.ds(0, 864)]
        down_ref[rows, :] = ref[:, pl.ds(896, 256)]
        down_ref[pl.ds(pl.multiple_of(place * 16 + 32, 16), 16), :] = ref[:, pl.ds(1152, 256)]


def coarse_kernel(xy_ref, own_ref, recv_ref, after_ref, out_ref):
    layer = lax.axis_index("morton")
    parity = layer % 2
    partner = layer + 1 - 2 * parity
    for target, half, ref in ((layer, parity, own_ref), (partner, 1 - parity, recv_ref)):
        pieces = jnp.concatenate([ref[:, wz * 128 : (wz + 1) * 128] for wz in range(HALF)], axis=0)
        key = octant_key(xy_ref, target, parity, iota((128, PLANE), 0))
        for q in range(2):
            lane = iota((128, PLANE), 1) + q * PLANE
            placed = mm(pieces, one_hot(key, lane)).astype(BF16)
            for wz in range(HALF):
                lanes = pl.ds(pl.multiple_of((half * HALF + wz) * PLANE, PLANE), PLANE)
                out_ref[q, :, lanes] = placed[wz * 64 : (wz + 1) * 64]


def call(body, name, out_shapes, operands, kinds, scratch=(), us=1, out_kinds=None, vmem_mib=24):
    specs = {"s": pl.BlockSpec(memory_space=pltpu.SMEM), "h": pl.BlockSpec(memory_space=pl.ANY)}
    specs["v"] = pl.BlockSpec(memory_space=pltpu.VMEM)
    single = not isinstance(out_shapes, list)
    out_specs = [specs[kind] for kind in out_kinds or "v" * (1 if single else len(out_shapes))]
    return pl.pallas_call(
        body,
        name=name,
        out_shape=out_shapes,
        in_specs=[specs[kind] for kind in kinds],
        out_specs=out_specs[0] if single else out_specs,
        scratch_shapes=list(scratch),
        compiler_params=pltpu.CompilerParams(vmem_limit_bytes=vmem_mib << 20),
        cost_estimate=pl.CostEstimate(flops=us * 10**9, bytes_accessed=us * 3500000, transcendentals=0),
    )(*operands)


def shape(dims, dtype=BF16):
    return jax.ShapeDtypeStruct(dims, dtype)


def exchange(value, bit):
    return lax.ppermute(value, "morton", [(i, i ^ (1 << bit)) for i in range(lax.axis_size("morton"))])


def exchange_cross(value):
    layers = lax.axis_size("morton")
    pairs = [(i, i + 1) for i in range(1, layers - 1, 2)]
    return lax.ppermute(value, "morton", pairs + [(target, source) for source, target in pairs])


def per_device(features, voxel_mask, brick_xy, neighbours, conv_weight, down_weight, coarse_grad):
    bricks, channels, voxels = features.shape
    layers = lax.axis_size("morton")
    rounds = layers.bit_length() - 1
    scale = 1.0 / math.sqrt(bricks * layers * voxels)
    side_shape = shape((32, 2 * PLANE))
    oct_shape = shape((64, 1024))
    xy = brick_xy.T
    block = shape((96, 288))
    core_edge, cross_edge, own, away, flipped, stacked, down_t = call(
        prepare_kernel, "prepare", [side_shape, side_shape, oct_shape, oct_shape, block, block, shape((64, 256))],
        (xy, features, voxel_mask, coarse_grad, conv_weight, down_weight), "shhhhh",
        scratch=[
            pltpu.VMEM((2, 2, 32, PLANE), BF16), pltpu.VMEM((2, 2, PLANE), I32),
            pltpu.VMEM((2, 2, 64, HALF * PLANE), BF16), pltpu.VMEM((32, 864), BF16), pltpu.VMEM((64, 256), BF16),
            pltpu.SemaphoreType.DMA((8,)),
        ],
        us=2, vmem_mib=58,
    )
    core_side = exchange(core_edge, 0)
    cross_side = exchange_cross(cross_edge)
    arrived = exchange(away, 0)
    acc_shape = shape((20 * 32, PLANE), F32)
    cols = pltpu.VMEM((16 * 288, PLANE), BF16)
    two_cols = pltpu.VMEM((2, 16 * 288, PLANE), BF16)
    mask = pltpu.VMEM((2, voxels), I32)
    windows = pltpu.VMEM((2, 9, 32, PLANE), BF16)
    all_cols, acc = call(
        inner_kernel, "forward_own_planes",
        [shape((2, 16 * 288, PLANE)), shape((2, 4096, PLANE), F32)],
        (xy, features, voxel_mask, stacked), "shhh", out_kinds="hh",
        scratch=[
            pltpu.VMEM((2, 32, voxels), BF16), mask, pltpu.VMEM((96, 288), BF16), pltpu.VMEM((2, 2, 9, 32, PLANE), BF16), pltpu.VMEM((512, 512), BF16),
            two_cols, pltpu.VMEM((2, 20 * 32, PLANE), F32), pltpu.SemaphoreType.DMA((7,)),
        ],
        us=5, vmem_mib=58,
    )
    octants, gplanes, gcore, gcross, sums = call(
        functools.partial(outer_kernel, layers, scale), "forward_rest",
        [oct_shape, shape((512, 512)), side_shape, side_shape, shape((32, 1408), F32)],
        (xy, all_cols, acc, voxel_mask, down_weight, core_side, cross_side, own, arrived, stacked, down_t), "shhhhvvvvvv",
        scratch=[
            two_cols, pltpu.VMEM((2, 512, PLANE), F32), mask, pltpu.VMEM((64, 256), BF16),
            pltpu.VMEM((512, 512), BF16), pltpu.VMEM((2, HALF, 256, PLANE), BF16), pltpu.VMEM((256, 1024), BF16),
            pltpu.VMEM((2, 20 * 32, PLANE), BF16), pltpu.VMEM((96, 288), F32), pltpu.SemaphoreType.DMA((4,)),
        ],
        us=6, vmem_mib=50,
    )
    odd = lax.axis_index("morton") % 2
    rows = sums.shape[0] // 2
    keep = lax.dynamic_slice_in_dim(sums, odd * rows, rows, 0)
    total = keep + exchange(lax.dynamic_slice_in_dim(sums, (1 - odd) * rows, rows, 0), 0)
    gcore_side = exchange(gcore, 0)
    octants_there = exchange(octants, 0)
    gcross_side = exchange_cross(gcross)
    back = []
    for bit in range(1, rounds):
        step = exchange(total, bit)
        if bit in (1, 2):
            back.append(
                call(
                    functools.partial(back_inner_kernel, bit - 1), "backward_own_planes", acc_shape,
                    (xy, total, gplanes, flipped), "shvv", scratch=[windows, cols], us=3,
                )
            )
        if bit == 3:
            input_grad = call(
                functools.partial(back_outer_kernel, layers), "backward_rest", shape((bricks, channels, voxels)),
                (xy, voxel_mask, total, *back, gcore_side, gcross_side, flipped), "shhvvvvv",
                scratch=[mask, pltpu.VMEM((2, 512, PLANE), F32), pltpu.SemaphoreType.DMA((1,))], us=2,
            )
        total = total + step
    other = exchange(total, 0)
    coarse_out = call(
        coarse_kernel, "place", shape((2, 64, voxels)), (xy, octants, octants_there, total), "svvh", us=2
    )
    conv_grad, down_grad = call(
        finish_kernel, "finish", [shape((32, 864), F32), shape((64, 256), F32)], (total, other), "vv"
    )
    return coarse_out, input_grad, conv_grad, down_grad


def solution(mesh):
    return jax.shard_map(
        per_device,
        mesh=mesh,
        in_specs=(
            P(("groups", "morton"), None, None),
            P(("groups", "morton"), None),
            P("groups", None),
            P(("groups", "morton"), None),
            P(),
            P(),
            P(("groups", "morton"), None, None),
        ),
        out_specs=(
            P(("groups", "morton"), None, None),
            P(("groups", "morton"), None, None),
            P("groups", None),
            P("groups", None),
        ),
        check_vma=False,
    )
```

```python
import functools
import math

import jax
import jax.numpy as jnp
from jax import lax
from jax.experimental import pallas as pl
from jax.experimental.pallas import tpu as pltpu
from jax.sharding import PartitionSpec as P

EDGE = 16
HALF = 8
PLANE = EDGE * EDGE
QUARTER = HALF * HALF
BF16 = jnp.bfloat16
F32 = jnp.float32
I32 = jnp.int32
STEP = 8


def iota(shape, dim):
    return lax.broadcasted_iota(I32, shape, dim)


def one_hot(row_key, column_key):
    return jnp.where(row_key == column_key, 1.0, 0.0).astype(BF16)


def mm(a, b):
    return jnp.dot(a, b, preferred_element_type=F32)


def mm_nt(a, b):
    return lax.dot_general(a, b, (((1,), (1,)), ((), ())), preferred_element_type=F32)


def xy_of(xy_ref, layer, brick):
    return xy_ref[0, layer * 2 + brick], xy_ref[1, layer * 2 + brick]


def octant_key(xy_ref, layer, parity, lane):
    brick = (lane >> 6) & 1
    bases = []
    for b in range(2):
        x, y = xy_of(xy_ref, layer, b)
        base = (x // 2) * PLANE + (y % 2) * HALF * EDGE + (x % 2) * HALF
        bases.append(jnp.where(y // 2 == parity, base, -65536))
    return jnp.where(brick == 0, bases[0], bases[1]) + ((lane >> 3) & 7) * EDGE + (lane & 7)


def start_all(pairs, sems):
    copies = [pltpu.make_async_copy(source, target, sems.at[i]) for i, (source, target) in enumerate(pairs)]
    for copy in copies:
        copy.start()
    return copies


def prepare_kernel(
    xy_ref, feat_hbm, mask_hbm, grad_hbm, weight_hbm, down_hbm,
    send_ref, cross_ref, own_ref, flipped_ref, stacked_ref, down_t_ref,
    feat_ref, mask_ref, grad_ref, weight_ref, down_ref, sems,
):
    layer = lax.axis_index("morton")
    parity = layer % 2
    partner = layer + 1 - 2 * parity
    halves = [
        grad_hbm.at[:, :, pl.ds(pl.multiple_of(half * HALF * PLANE, HALF * PLANE), HALF * PLANE)]
        for half in (1 - parity, parity)
    ]
    pairs = [(weight_hbm, weight_ref), (down_hbm, down_ref)]
    for side in range(2):
        z = jnp.where(parity == side, EDGE - 1, 0)
        lanes = pl.ds(pl.multiple_of(z * PLANE, PLANE), PLANE)
        pairs += [(feat_hbm.at[:, :, lanes], feat_ref.at[side]), (mask_hbm.at[:, lanes], mask_ref.at[side])]
    pairs += [(halves[0], grad_ref.at[0]), (halves[1], grad_ref.at[1])]
    copies = start_all(pairs, sems)
    row = iota((2 * PLANE, 2 * QUARTER), 0)
    lane = iota((2 * PLANE, 2 * QUARTER), 1)
    picks = [one_hot(row, octant_key(xy_ref, target, parity, lane)) for target in (partner, layer)]
    for copy in copies[:2]:
        copy.wait()
    flipped = weight_ref[...].astype(F32).T.astype(BF16)
    for dz in range(3):
        rows = pl.ds(dz * 32, 32)
        blocks = [flipped[j * 32 : (j + 1) * 32] for j in (26 - dz * 9 - s for s in range(9))]
        flipped_ref[rows, :] = jnp.concatenate(blocks, axis=1)
        stacked_ref[rows, :] = weight_ref[:, pl.ds(dz * 288, 288)]
    down_t = down_ref[...].astype(F32).T.astype(BF16)
    for kz in range(2):
        blocks = [down_t[(kz * 4 + k) * 32 : (kz * 4 + k + 1) * 32] for k in range(4)]
        down_t_ref[pl.ds(kz * 32, 32), :] = jnp.concatenate(blocks, axis=1)
    for copy in copies[2:6]:
        copy.wait()
    for side, ref in enumerate((send_ref.at[pl.ds(64, 32)], cross_ref)):
        for r in range(2):
            mask = mask_ref[side, pl.ds(r, 1), :].astype(F32).astype(BF16)
            ref[:, pl.ds(r * PLANE, PLANE)] = feat_ref[side, r] * mask
    for i, ref in enumerate((send_ref.at[pl.ds(0, 64)], own_ref)):
        copies[6 + i].wait()
        planes = [
            jnp.concatenate([grad_ref[i, q, :, pl.ds(wz * PLANE, PLANE)] for q in range(2)], axis=1) for wz in range(HALF)
        ]
        found = mm(jnp.concatenate(planes, axis=0), picks[i]).astype(BF16)
        for wz in range(HALF):
            ref[:, pl.ds(wz * 2 * QUARTER, 2 * QUARTER)] = found[wz * 64 : (wz + 1) * 64]


def window_mask(shift, ox, oy):
    dy, dx = shift // 3 - 1, shift % 3 - 1
    voxel = (iota((1, PLANE), 1) - (EDGE * dy + dx)) & (PLANE - 1)
    x = (voxel & (EDGE - 1)) + dx - EDGE * ox
    y = (voxel >> 4) + dy - EDGE * oy
    inside = jnp.where(((x | y) & -EDGE) == 0, 1.0, 0.0)
    return jnp.broadcast_to(inside, (32, PLANE)).astype(BF16)


def offset_of(xy_ref, layer, r, other, s):
    x, y = xy_of(xy_ref, layer, r)
    near_x, near_y = xy_of(xy_ref, other, s)
    return near_x - x, near_y - y


def turned(planes, ox):
    return pltpu.roll(planes, (ox * EDGE) & (PLANE - 1), 1)


def shifted(first, second, masks, shift):
    dy, dx = shift // 3 - 1, shift % 3 - 1
    times = first.shape[0] // 32
    both = first * jnp.tile(masks[0], (times, 1)) + second * jnp.tile(masks[1], (times, 1))
    back = (-(EDGE * dy + dx)) & (PLANE - 1)
    return pltpu.roll(both, back, 1) if back else both


def build_masks(ox, oy, rows_ref, mask_ref):
    shift = iota((16, PLANE), 0)
    dy = (shift >= 3).astype(I32) + (shift >= 6).astype(I32) - 1
    dx = shift - 3 * dy - 4
    voxel = (iota((16, PLANE), 1) - (EDGE * dy + dx)) & (PLANE - 1)
    x = (voxel & (EDGE - 1)) + dx - EDGE * ox
    y = (voxel >> 4) + dy - EDGE * oy
    rows_ref[...] = jnp.where(((x | y) & -EDGE) == 0, 1.0, 0.0)
    for s in range(9):
        mask_ref[s] = jnp.broadcast_to(rows_ref[pl.ds(s, 1), :], (32, PLANE)).astype(BF16)


def unfold_planes(planes_ref, r, first, ox, own_ref, other_ref, cols_ref):
    for p in range(first, first + STEP, STEP):
        rows = pl.ds(p * 32, STEP * 32)
        own = planes_ref[rows, pl.ds(r * PLANE, PLANE)]
        other = turned(planes_ref[rows, pl.ds((1 - r) * PLANE, PLANE)], ox)
        for shift in range(9):
            piece = own if shift == 4 else shifted(own, other, (own_ref[shift], other_ref[shift]), shift)
            for q in range(STEP):
                cols_ref[pl.ds((p + q) * 288 + shift * 32, 32), :] = piece[q * 32 : (q + 1) * 32]


def unfold_side(xy_ref, layer, r, other, planes):
    places = [offset_of(xy_ref, layer, r, other, s) for s in range(2)]
    first, second = (turned(planes[:, s * PLANE : (s + 1) * PLANE], places[s][0]) for s in range(2))
    pieces = []
    for shift in range(9):
        masks = [window_mask(shift, ox, oy) for ox, oy in places]
        pieces.append(shifted(first, second, masks, shift))
    return jnp.concatenate(pieces, axis=0)


def convolve(stacked, cols_ref, acc_ref):
    acc_ref[...] = jnp.zeros(acc_ref.shape, F32)
    for p in range(EDGE):
        rows = pl.ds((EDGE - p) * 32, 96)
        acc_ref[rows, :] += mm(stacked, cols_ref[pl.ds(p * 288, 288), :])


def inner_kernel(
    xy_ref, feat_hbm, mask_hbm, stacked_hbm, cols_hbm, acc_hbm,
    feat_ref, mask_ref, stacked_ref, rows_ref, window_ref, in_ref, cols_ref, acc_ref, sems,
):
    layer = lax.axis_index("morton")
    copies = start_all(((feat_hbm, feat_ref), (mask_hbm, mask_ref), (stacked_hbm, stacked_ref)), sems)
    build_masks(0, 0, rows_ref, window_ref.at[2])
    ox = []
    for r in range(2):
        x, y = offset_of(xy_ref, layer, r, layer, 1 - r)
        build_masks(x, y, rows_ref, window_ref.at[r])
        ox.append(x)
    for copy in copies:
        copy.wait()
    for r in range(2):
        for z in range(EDGE):
            lanes = pl.ds(z * PLANE, PLANE)
            mask = mask_ref[pl.ds(r, 1), lanes].astype(F32).astype(BF16)
            in_ref[pl.ds(z * 32, 32), pl.ds(r * PLANE, PLANE)] = feat_ref[r, :, lanes] * mask
    out = []
    for r in range(2):
        for i in range(2):
            unfold_planes(in_ref, r, i * STEP, ox[r], window_ref.at[2], window_ref.at[r], cols_ref.at[r])
            rows = pl.ds(i * STEP * 288, STEP * 288)
            out += start_all(((cols_ref.at[r, rows], cols_hbm.at[r, rows]),), sems.at[pl.ds(5 + 2 * r + i, 1)])
    for r in range(2):
        convolve(stacked_ref[...], cols_ref.at[r], acc_ref.at[r])
        out += start_all(((acc_ref.at[r, pl.ds(64, 512)], acc_hbm.at[r, pl.ds(0, 512)]),), sems.at[pl.ds(3 + r, 1)])
    for copy in out:
        copy.wait()


def sides_of(layer, layers):
    odd = layer % 2
    above = layer + 1 - odd
    core = jnp.where(odd == 0, layer + 1, layer - 1)
    cross = jnp.where(odd == 0, jnp.maximum(layer - 1, 0), jnp.minimum(layer + 1, layers - 1))
    return ((core, 2 * (1 - odd), 15 * (1 - odd)), (cross, 2 * odd, 15 * odd))


def rows_at(index):
    return pl.ds(pl.multiple_of(index * 32, 32), 32)


def outer_kernel(
    layers, scale, xy_ref, cols_hbm, acc_hbm, mask_hbm, down_hbm, recv_ref, cross_ref, own_ref, stacked_ref, down_t_ref,
    message_ref, gplanes_ref, gcross_ref, small_ref, sums_ref,
    cols_ref, acc_ref, mask_ref, down_ref, gather_ref, act_ref, up_ref, stride_ref, grad_ref, total_ref, sems,
):
    copies = start_all(
        ((acc_hbm.at[:, pl.ds(0, 512)], acc_ref), (mask_hbm, mask_ref), (down_hbm, down_ref), (cols_hbm, cols_ref)), sems
    )
    layer = lax.axis_index("morton")
    sides = sides_of(layer, layers)

    row = iota((2 * PLANE, PLANE), 0)
    lane = iota((2 * PLANE, PLANE), 1)
    row_key = (row >> 8) * 4096 + ((row >> 4) & 15) * 64 + (row & 15)
    lane_key = ((lane >> 6) & 1) * 4096 + ((lane >> 3) & 7) * 128 + (lane & 7) * 2 + (lane >> 7)
    for ky in range(2):
        gather_ref[ky] = one_hot(row_key, lane_key + ky * 64)

    core_ref = recv_ref.at[pl.ds(64, 32), pl.ds(0, 2 * PLANE)]
    oct_ref = message_ref.at[pl.ds(0, 64)]
    gcore_ref = message_ref.at[pl.ds(64, 32), pl.ds(0, 2 * PLANE)]
    grad_oct = own_ref[...] + recv_ref[pl.ds(0, 64), :]
    pieces = jnp.concatenate([grad_oct[:, wz * 128 : (wz + 1) * 128] for wz in range(HALF)], axis=0)
    row = iota((128, PLANE), 0)
    lane = iota((128, PLANE), 1)
    parities = []
    for k in range(4):
        voxel = iota((1, PLANE), 1)
        hit = jnp.where(((voxel >> 4) & 1) * 2 + (voxel & 1) == k, 1.0, 0.0)
        parities.append(jnp.broadcast_to(hit, (64, PLANE)).astype(BF16))
    for r in range(2):
        row_key = jnp.where((row >> 6) == r, row & 63, -1)
        spread = mm(pieces, one_hot(row_key, (lane >> 5) * HALF + ((lane >> 1) & 7))).astype(BF16)
        for wz in range(HALF):
            for k in range(4):
                up_ref[r, wz, pl.ds(k * 64, 64), :] = spread[wz * 64 : (wz + 1) * 64] * parities[k]
    side_cols = []
    for (other, dz, z), ref in zip(sides, (core_ref, cross_ref)):
        for r in range(2):
            side_cols.append(unfold_side(xy_ref, layer, r, other, ref[...]))
    for copy in copies[:3]:
        copy.wait()
    small_ref[...] = mask_ref[...].astype(F32).astype(BF16)
    for side, (other, dz, z) in enumerate(sides):
        for r in range(2):
            acc_ref[r, rows_at(15 - z), :] += mm(stacked_ref[rows_at(dz), :], side_cols[side * 2 + r])
    zeros = jnp.zeros((64, PLANE), BF16)
    for r in range(2):
        grad_ref[r, pl.ds(0, 64), :] = zeros
        grad_ref[r, pl.ds(18 * 32, 64), :] = zeros
        for wz in range(HALF):
            grad_act = mm(down_t_ref[...], up_ref[r, wz])
            for kz in range(2):
                z = 2 * wz + kz
                mask = mask_ref[pl.ds(r, 1), pl.ds(z * PLANE, PLANE)].astype(F32)
                pre = acc_ref[r, pl.ds((15 - z) * 32, 32), :]
                sig = 1.0 / (1.0 + jnp.exp(-pre))
                masked = sig * mask
                act_ref[pl.ds(z * 32, 32), pl.ds(r * PLANE, PLANE)] = (pre * masked).astype(BF16)
                grad = grad_act[kz * 32 : (kz + 1) * 32] * masked * (1.0 + pre * (1.0 - sig))
                grad = grad.astype(BF16)
                grad_ref[r, pl.ds((17 - z) * 32, 32), :] = grad
                gplanes_ref[pl.ds(z * 32, 32), pl.ds(r * PLANE, PLANE)] = grad
        for (other, dz, z), ref in zip(sides, (gcore_ref, gcross_ref)):
            ref[:, pl.ds(r * PLANE, PLANE)] = grad_ref[r, rows_at(17 - z), :]

    for ky in range(2):
        found = mm(act_ref[...], gather_ref[ky]).astype(BF16)
        for z in range(EDGE):
            for kx in range(2):
                rows = pl.ds((z % 2) * 128 + (ky * 2 + kx) * 32, 32)
                stride_ref[rows, pl.ds((z // 2) * 128, 128)] = found[z * 32 : (z + 1) * 32, kx * 128 : (kx + 1) * 128]
    oct_ref[...] = mm(down_ref[...], stride_ref[...]).astype(BF16)
    down_sum = mm_nt(grad_oct, stride_ref[...]) * scale
    sums_ref[:, pl.ds(896, 256)] = down_sum[:32]
    sums_ref[:, pl.ds(1152, 256)] = down_sum[32:]

    copies[3].wait()
    total = jnp.zeros((288, 96), F32)
    for r in range(2):
        for p in range(EDGE):
            total += mm_nt(cols_ref[r, pl.ds(p * 288, 288), :], grad_ref[r, pl.ds((EDGE - p) * 32, 96), :])
    total_ref[...] = total.T
    for side, (other, dz, z) in enumerate(sides):
        for r in range(2):
            total_ref[rows_at(dz), :] += mm_nt(grad_ref[r, rows_at(17 - z), :], side_cols[side * 2 + r])
    total = [total_ref[pl.ds(dz * 32, 32), :] for dz in range(3)]
    sums_ref[:, pl.ds(0, 896)] = jnp.concatenate([*total, jnp.zeros((32, 32), F32)], axis=1) * scale


def back_inner_kernel(xy_ref, after_ref, gplanes_ref, flipped_ref, acc_ref, rows_ref, window_ref, cols_ref):
    layer = lax.axis_index("morton")
    build_masks(0, 0, rows_ref, window_ref.at[0])
    for r in range(2):
        ox, oy = offset_of(xy_ref, layer, r, layer, 1 - r)
        build_masks(ox, oy, rows_ref, window_ref.at[1 + r])
        for i in range(2):
            unfold_planes(gplanes_ref, r, i * STEP, ox, window_ref.at[0], window_ref.at[1 + r], cols_ref.at[r])
        convolve(flipped_ref[...], cols_ref.at[r], acc_ref.at[r])


def back_outer_kernel(layers, xy_ref, mask_ref, after_ref, acc_ref, recv_ref, cross_ref, flipped_ref, out_hbm, out_ref, sems):
    core_ref = recv_ref.at[pl.ds(64, 32), pl.ds(0, 2 * PLANE)]
    layer = lax.axis_index("morton")
    odd = layer % 2
    out = []
    for r in range(2):
        terms = []
        for (other, dz, z), ref in zip(sides_of(layer, layers), (core_ref, cross_ref)):
            terms.append(mm(flipped_ref[rows_at(dz), :], unfold_side(xy_ref, layer, r, other, ref[...])))
        below = jnp.where(odd == 1, terms[0], terms[1])
        above = jnp.where(odd == 1, terms[1], terms[0])
        for z in range(EDGE):
            lanes = pl.ds(z * PLANE, PLANE)
            mask = mask_ref[pl.ds(r, 1), lanes].astype(F32)
            grad = acc_ref[r, pl.ds((17 - z) * 32, 32), :]
            if z == 0:
                grad = grad + below
            if z == EDGE - 1:
                grad = grad + above
            out_ref[r, :, lanes] = (grad * mask).astype(BF16)
        out += start_all(((out_ref.at[r], out_hbm.at[r]),), sems.at[pl.ds(r, 1)])
    for copy in out:
        copy.wait()


def finish_kernel(total_ref, other_ref, conv_ref, down_ref):
    odd = lax.axis_index("morton") % 2
    for place, ref in ((odd, total_ref), (1 - odd, other_ref)):
        rows = pl.ds(pl.multiple_of(place * 16, 16), 16)
        conv_ref[rows, :] = ref[:, pl.ds(0, 864)]
        down_ref[rows, :] = ref[:, pl.ds(896, 256)]
        down_ref[pl.ds(pl.multiple_of(place * 16 + 32, 16), 16), :] = ref[:, pl.ds(1152, 256)]


def coarse_kernel(xy_ref, own_ref, recv_ref, after_ref, out_hbm, out_ref, sems):
    layer = lax.axis_index("morton")
    parity = layer % 2
    partner = layer + 1 - 2 * parity
    out = []
    for i, (target, half, ref) in enumerate(((layer, parity, own_ref), (partner, 1 - parity, recv_ref))):
        pieces = jnp.concatenate([ref[:64, wz * 128 : (wz + 1) * 128] for wz in range(HALF)], axis=0)
        key = octant_key(xy_ref, target, parity, iota((128, 2 * PLANE), 0))
        placed = mm(pieces, one_hot(key, iota((128, 2 * PLANE), 1))).astype(BF16)
        for q in range(2):
            for wz in range(HALF):
                out_ref[i, q, :, pl.ds(wz * PLANE, PLANE)] = placed[wz * 64 : (wz + 1) * 64, q * PLANE : (q + 1) * PLANE]
        lanes = pl.ds(pl.multiple_of(half * HALF * PLANE, HALF * PLANE), HALF * PLANE)
        out += start_all(((out_ref.at[i], out_hbm.at[:, :, lanes]),), sems.at[pl.ds(i, 1)])
    for copy in out:
        copy.wait()


def call(body, name, out_shapes, operands, kinds, scratch=(), us=1, out_kinds=None, vmem_mib=24):
    specs = {"s": pl.BlockSpec(memory_space=pltpu.SMEM), "h": pl.BlockSpec(memory_space=pl.ANY)}
    specs["v"] = pl.BlockSpec(memory_space=pltpu.VMEM)
    single = not isinstance(out_shapes, list)
    out_specs = [specs[kind] for kind in out_kinds or "v" * (1 if single else len(out_shapes))]
    return pl.pallas_call(
        body,
        name=name,
        out_shape=out_shapes,
        in_specs=[specs[kind] for kind in kinds],
        out_specs=out_specs[0] if single else out_specs,
        scratch_shapes=list(scratch),
        compiler_params=pltpu.CompilerParams(vmem_limit_bytes=vmem_mib << 20),
        cost_estimate=pl.CostEstimate(flops=us * 10**9, bytes_accessed=us * 3500000, transcendentals=0),
    )(*operands)


def shape(dims, dtype=BF16):
    return jax.ShapeDtypeStruct(dims, dtype)


def exchange(value, bit):
    return lax.ppermute(value, "morton", [(i, i ^ (1 << bit)) for i in range(lax.axis_size("morton"))])


def exchange_cross(value):
    layers = lax.axis_size("morton")
    pairs = [(i, i + 1) for i in range(1, layers - 1, 2)]
    return lax.ppermute(value, "morton", pairs + [(target, source) for source, target in pairs])


def per_device(features, voxel_mask, brick_xy, neighbours, conv_weight, down_weight, coarse_grad):
    bricks, channels, voxels = features.shape
    layers = lax.axis_size("morton")
    rounds = layers.bit_length() - 1
    scale = 1.0 / math.sqrt(bricks * layers * voxels)
    side_shape = shape((32, 2 * PLANE))
    oct_shape = shape((64, 1024))
    message_shape = shape((96, 1024))
    xy = brick_xy.T
    block = shape((96, 288))
    message, cross_edge, own, flipped, stacked, down_t = call(
        prepare_kernel, "prepare", [message_shape, side_shape, oct_shape, block, block, shape((64, 256))],
        (xy, features, voxel_mask, coarse_grad, conv_weight, down_weight), "shhhhh",
        scratch=[
            pltpu.VMEM((2, 2, 32, PLANE), BF16), pltpu.VMEM((2, 2, PLANE), I32),
            pltpu.VMEM((2, 2, 64, HALF * PLANE), BF16), pltpu.VMEM((32, 864), BF16), pltpu.VMEM((64, 256), BF16),
            pltpu.SemaphoreType.DMA((8,)),
        ],
        us=2, vmem_mib=58,
    )
    arrived = exchange(message, 0)
    cross_side = exchange_cross(cross_edge)
    two_cols = pltpu.VMEM((2, 16 * 288, PLANE), BF16)
    mask = pltpu.VMEM((2, voxels), I32)
    windows = pltpu.VMEM((3, 9, 32, PLANE), BF16)
    mask_rows = pltpu.VMEM((16, PLANE), F32)
    all_cols, acc = call(
        inner_kernel, "forward_own_planes",
        [shape((2, 16 * 288, PLANE)), shape((2, 4096, PLANE), F32)],
        (xy, features, voxel_mask, stacked), "shhh", out_kinds="hh",
        scratch=[
            pltpu.VMEM((2, 32, voxels), BF16), mask, pltpu.VMEM((96, 288), BF16), mask_rows, windows,
            pltpu.VMEM((512, 512), BF16),
            two_cols, pltpu.VMEM((2, 20 * 32, PLANE), F32), pltpu.SemaphoreType.DMA((9,)),
        ],
        us=5, vmem_mib=58,
    )
    message, gplanes, gcross, small_mask, sums = call(
        functools.partial(outer_kernel, layers, scale), "forward_rest",
        [message_shape, shape((512, 512)), side_shape, shape((2, voxels)), shape((32, 1408), F32)],
        (xy, all_cols, acc, voxel_mask, down_weight, arrived, cross_side, own, stacked, down_t), "shhhhvvvvv",
        scratch=[
            two_cols, pltpu.VMEM((2, 512, PLANE), F32), mask, pltpu.VMEM((64, 256), BF16),
            pltpu.VMEM((2, 512, PLANE), BF16), pltpu.VMEM((512, 512), BF16), pltpu.VMEM((2, HALF, 256, PLANE), BF16), pltpu.VMEM((256, 1024), BF16),
            pltpu.VMEM((2, 20 * 32, PLANE), BF16), pltpu.VMEM((96, 288), F32), pltpu.SemaphoreType.DMA((4,)),
        ],
        us=6, vmem_mib=50,
    )
    odd = lax.axis_index("morton") % 2
    rows = sums.shape[0] // 2
    keep = lax.dynamic_slice_in_dim(sums, odd * rows, rows, 0)
    total = keep + exchange(lax.dynamic_slice_in_dim(sums, (1 - odd) * rows, rows, 0), 0)
    message_there = exchange(message, 0)
    for bit in range(1, rounds):
        if bit < 2:
            sent = total
            step = exchange(sent, bit)
        else:
            sent = lax.reduce_precision(total, 8, 7)
            step = exchange(sent.astype(BF16), bit).astype(F32)
        if bit == 1:
            gcross, _ = lax.optimization_barrier((gcross, total))
            gcross_side = exchange_cross(gcross)
        if bit == 2:
            back = call(
                back_inner_kernel, "backward_own_planes", shape((2, 20 * 32, PLANE), F32),
                (xy, total, gplanes, flipped), "shvv", scratch=[mask_rows, windows, two_cols], us=3,
            )
        if bit == 3:
            input_grad = call(
                functools.partial(back_outer_kernel, layers), "backward_rest", shape((bricks, channels, voxels)),
                (xy, small_mask, total, back, message_there, gcross_side, flipped), "svhvvvv", out_kinds="h",
                scratch=[pltpu.VMEM((bricks, channels, voxels), BF16), pltpu.SemaphoreType.DMA((2,))], us=2,
            )
        total = sent + step
    other = exchange(total, 0)
    coarse_out = call(
        coarse_kernel, "place", shape((2, 64, voxels)), (xy, message, message_there, total), "svvh", out_kinds="h",
        scratch=[pltpu.VMEM((2, 2, 64, HALF * PLANE), BF16), pltpu.SemaphoreType.DMA((2,))], us=2,
    )
    conv_grad, down_grad = call(
        finish_kernel, "finish", [shape((32, 864), F32), shape((64, 256), F32)], (total, other), "vv"
    )
    return coarse_out, input_grad, conv_grad, down_grad


def solution(mesh):
    return jax.shard_map(
        per_device,
        mesh=mesh,
        in_specs=(
            P(("groups", "morton"), None, None),
            P(("groups", "morton"), None),
            P("groups", None),
            P(("groups", "morton"), None),
            P(),
            P(),
            P(("groups", "morton"), None, None),
        ),
        out_specs=(
            P(("groups", "morton"), None, None),
            P(("groups", "morton"), None, None),
            P("groups", None),
            P("groups", None),
        ),
        check_vma=False,
    )
```

```python
import functools
import math

import jax
import jax.numpy as jnp
from jax import lax
from jax.experimental import pallas as pl
from jax.experimental.pallas import tpu as pltpu
from jax.sharding import PartitionSpec as P

EDGE = 16
HALF = 8
PLANE = EDGE * EDGE
QUARTER = HALF * HALF
BF16 = jnp.bfloat16
F32 = jnp.float32
I32 = jnp.int32
STEP = 8


def iota(shape, dim):
    return lax.broadcasted_iota(I32, shape, dim)


def one_hot(row_key, column_key):
    return jnp.where(row_key == column_key, 1.0, 0.0).astype(BF16)


def mm(a, b):
    return jnp.dot(a, b, preferred_element_type=F32)


def mm_nt(a, b):
    return lax.dot_general(a, b, (((1,), (1,)), ((), ())), preferred_element_type=F32)


def xy_of(xy_ref, layer, brick):
    return xy_ref[0, layer * 2 + brick], xy_ref[1, layer * 2 + brick]


def octant_key(xy_ref, layer, parity, lane):
    brick = (lane >> 6) & 1
    bases = []
    for b in range(2):
        x, y = xy_of(xy_ref, layer, b)
        base = (x // 2) * PLANE + (y % 2) * HALF * EDGE + (x % 2) * HALF
        bases.append(jnp.where(y // 2 == parity, base, -65536))
    return jnp.where(brick == 0, bases[0], bases[1]) + ((lane >> 3) & 7) * EDGE + (lane & 7)


def start_all(pairs, sems):
    copies = [pltpu.make_async_copy(source, target, sems.at[i]) for i, (source, target) in enumerate(pairs)]
    for copy in copies:
        copy.start()
    return copies


def prepare_kernel(
    xy_ref, feat_hbm, mask_hbm, grad_hbm, weight_hbm, down_hbm,
    send_ref, cross_ref, own_ref, flipped_ref, stacked_ref, down_t_ref,
    feat_ref, mask_ref, grad_ref, weight_ref, down_ref, sems,
):
    layer = lax.axis_index("morton")
    parity = layer % 2
    partner = layer + 1 - 2 * parity
    halves = [
        grad_hbm.at[:, :, pl.ds(pl.multiple_of(half * HALF * PLANE, HALF * PLANE), HALF * PLANE)]
        for half in (1 - parity, parity)
    ]
    pairs = [(weight_hbm, weight_ref), (down_hbm, down_ref)]
    for side in range(2):
        z = jnp.where(parity == side, EDGE - 1, 0)
        lanes = pl.ds(pl.multiple_of(z * PLANE, PLANE), PLANE)
        pairs += [(feat_hbm.at[:, :, lanes], feat_ref.at[side]), (mask_hbm.at[:, lanes], mask_ref.at[side])]
    pairs += [(halves[0], grad_ref.at[0]), (halves[1], grad_ref.at[1])]
    copies = start_all(pairs, sems)
    row = iota((2 * PLANE, 2 * QUARTER), 0)
    lane = iota((2 * PLANE, 2 * QUARTER), 1)
    picks = [one_hot(row, octant_key(xy_ref, target, parity, lane)) for target in (partner, layer)]
    for copy in copies[:2]:
        copy.wait()
    flipped = weight_ref[...].astype(F32).T.astype(BF16)
    for dz in range(3):
        rows = pl.ds(dz * 32, 32)
        blocks = [flipped[j * 32 : (j + 1) * 32] for j in (26 - dz * 9 - s for s in range(9))]
        flipped_ref[rows, :] = jnp.concatenate(blocks, axis=1)
        stacked_ref[rows, :] = weight_ref[:, pl.ds(dz * 288, 288)]
    down_t = down_ref[...].astype(F32).T.astype(BF16)
    for kz in range(2):
        blocks = [down_t[(kz * 4 + k) * 32 : (kz * 4 + k + 1) * 32] for k in range(4)]
        down_t_ref[pl.ds(kz * 32, 32), :] = jnp.concatenate(blocks, axis=1)
    for copy in copies[2:6]:
        copy.wait()
    for side, ref in enumerate((send_ref.at[pl.ds(64, 32)], cross_ref)):
        for r in range(2):
            mask = mask_ref[side, pl.ds(r, 1), :].astype(F32).astype(BF16)
            ref[:, pl.ds(r * PLANE, PLANE)] = feat_ref[side, r] * mask
    for i, ref in enumerate((send_ref.at[pl.ds(0, 64)], own_ref)):
        copies[6 + i].wait()
        planes = [
            jnp.concatenate([grad_ref[i, q, :, pl.ds(wz * PLANE, PLANE)] for q in range(2)], axis=1) for wz in range(HALF)
        ]
        found = mm(jnp.concatenate(planes, axis=0), picks[i]).astype(BF16)
        for wz in range(HALF):
            ref[:, pl.ds(wz * 2 * QUARTER, 2 * QUARTER)] = found[wz * 64 : (wz + 1) * 64]


def window_mask(shift, ox, oy):
    dy, dx = shift // 3 - 1, shift % 3 - 1
    voxel = (iota((1, PLANE), 1) - (EDGE * dy + dx)) & (PLANE - 1)
    x = (voxel & (EDGE - 1)) + dx - EDGE * ox
    y = (voxel >> 4) + dy - EDGE * oy
    inside = jnp.where(((x | y) & -EDGE) == 0, 1.0, 0.0)
    return jnp.broadcast_to(inside, (32, PLANE)).astype(BF16)


def offset_of(xy_ref, layer, r, other, s):
    x, y = xy_of(xy_ref, layer, r)
    near_x, near_y = xy_of(xy_ref, other, s)
    return near_x - x, near_y - y


def turned(planes, ox):
    return pltpu.roll(planes, (ox * EDGE) & (PLANE - 1), 1)


def shifted(first, second, masks, shift):
    dy, dx = shift // 3 - 1, shift % 3 - 1
    times = first.shape[0] // 32
    both = first * jnp.tile(masks[0], (times, 1)) + second * jnp.tile(masks[1], (times, 1))
    back = (-(EDGE * dy + dx)) & (PLANE - 1)
    return pltpu.roll(both, back, 1) if back else both


def build_masks(ox, oy, rows_ref, mask_ref):
    shift = iota((16, PLANE), 0)
    dy = (shift >= 3).astype(I32) + (shift >= 6).astype(I32) - 1
    dx = shift - 3 * dy - 4
    voxel = (iota((16, PLANE), 1) - (EDGE * dy + dx)) & (PLANE - 1)
    x = (voxel & (EDGE - 1)) + dx - EDGE * ox
    y = (voxel >> 4) + dy - EDGE * oy
    rows_ref[...] = jnp.where(((x | y) & -EDGE) == 0, 1.0, 0.0)
    for s in range(9):
        mask_ref[s] = jnp.broadcast_to(rows_ref[pl.ds(s, 1), :], (32, PLANE)).astype(BF16)


def unfold_planes(planes_ref, r, first, ox, own_ref, other_ref, cols_ref):
    for p in range(first, first + STEP, STEP):
        rows = pl.ds(p * 32, STEP * 32)
        own = planes_ref[rows, pl.ds(r * PLANE, PLANE)]
        other = turned(planes_ref[rows, pl.ds((1 - r) * PLANE, PLANE)], ox)
        for shift in range(9):
            piece = own if shift == 4 else shifted(own, other, (own_ref[shift], other_ref[shift]), shift)
            for q in range(STEP):
                cols_ref[pl.ds((p + q) * 288 + shift * 32, 32), :] = piece[q * 32 : (q + 1) * 32]


def unfold_side(xy_ref, layers, layer, r, other, planes):
    valid = (other >= 0) & (other < layers)
    near = jnp.clip(other, 0, layers - 1)
    places = [offset_of(xy_ref, layer, r, near, s) for s in range(2)]
    places = [(jnp.where(valid, ox, 8), oy) for ox, oy in places]
    first, second = (turned(planes[:, s * PLANE : (s + 1) * PLANE], places[s][0]) for s in range(2))
    pieces = []
    for shift in range(9):
        masks = [window_mask(shift, ox, oy) for ox, oy in places]
        pieces.append(shifted(first, second, masks, shift))
    return jnp.concatenate(pieces, axis=0)


def convolve(stacked, cols_ref, acc_ref):
    acc_ref[...] = jnp.zeros(acc_ref.shape, F32)
    for p in range(EDGE):
        rows = pl.ds((EDGE - p) * 32, 96)
        acc_ref[rows, :] += mm(stacked, cols_ref[pl.ds(p * 288, 288), :])


def inner_kernel(
    xy_ref, feat_ref, mask_ref, stacked_ref, cols_hbm, acc_hbm, rows_ref, window_ref, in_ref, cols_ref, acc_ref, sems,
):
    layer = lax.axis_index("morton")
    build_masks(0, 0, rows_ref, window_ref.at[2])
    ox = []
    for r in range(2):
        x, y = offset_of(xy_ref, layer, r, layer, 1 - r)
        build_masks(x, y, rows_ref, window_ref.at[r])
        ox.append(x)
    for r in range(2):
        for z in range(EDGE):
            lanes = pl.ds(z * PLANE, PLANE)
            mask = mask_ref[pl.ds(r, 1), lanes].astype(F32).astype(BF16)
            in_ref[pl.ds(z * 32, 32), pl.ds(r * PLANE, PLANE)] = feat_ref[r, :, lanes] * mask
    out = []
    for r in range(2):
        for i in range(2):
            unfold_planes(in_ref, r, i * STEP, ox[r], window_ref.at[2], window_ref.at[r], cols_ref.at[r])
            rows = pl.ds(i * STEP * 288, STEP * 288)
            out += start_all(((cols_ref.at[r, rows], cols_hbm.at[r, rows]),), sems.at[pl.ds(2 + 2 * r + i, 1)])
    for r in range(2):
        convolve(stacked_ref[...], cols_ref.at[r], acc_ref.at[r])
        out += start_all(((acc_ref.at[r, pl.ds(64, 512)], acc_hbm.at[r, pl.ds(0, 512)]),), sems.at[pl.ds(r, 1)])
    for copy in out:
        copy.wait()


def sides_of(layer):
    odd = layer % 2
    core = jnp.where(odd == 0, layer + 1, layer - 1)
    cross = jnp.where(odd == 0, layer - 1, layer + 1)
    return ((core, 2 * (1 - odd), 15 * (1 - odd)), (cross, 2 * odd, 15 * odd))


def rows_at(index):
    return pl.ds(pl.multiple_of(index * 32, 32), 32)


def outer_kernel(
    layers, scale, xy_ref, cols_hbm, acc_hbm, mask_hbm, down_hbm, recv_ref, cross_ref, own_ref, stacked_ref, down_t_ref,
    message_ref, gplanes_ref, gcross_ref, small_ref, sums_ref,
    cols_ref, acc_ref, mask_ref, down_ref, gather_ref, act_ref, up_ref, stride_ref, grad_ref, total_ref, sems,
):
    copies = start_all(
        ((acc_hbm.at[:, pl.ds(0, 512)], acc_ref), (mask_hbm, mask_ref), (down_hbm, down_ref), (cols_hbm, cols_ref)), sems
    )
    layer = lax.axis_index("morton")
    sides = sides_of(layer)

    row = iota((2 * PLANE, PLANE), 0)
    lane = iota((2 * PLANE, PLANE), 1)
    row_key = (row >> 8) * 4096 + ((row >> 4) & 15) * 64 + (row & 15)
    lane_key = ((lane >> 6) & 1) * 4096 + ((lane >> 3) & 7) * 128 + (lane & 7) * 2 + (lane >> 7)
    for ky in range(2):
        gather_ref[ky] = one_hot(row_key, lane_key + ky * 64)

    core_ref = recv_ref.at[pl.ds(64, 32), pl.ds(0, 2 * PLANE)]
    oct_ref = message_ref.at[pl.ds(0, 64)]
    gcore_ref = message_ref.at[pl.ds(64, 32), pl.ds(0, 2 * PLANE)]
    grad_oct = own_ref[...] + recv_ref[pl.ds(0, 64), :]
    pieces = jnp.concatenate([grad_oct[:, wz * 128 : (wz + 1) * 128] for wz in range(HALF)], axis=0)
    row = iota((128, PLANE), 0)
    lane = iota((128, PLANE), 1)
    parities = []
    for k in range(4):
        voxel = iota((1, PLANE), 1)
        hit = jnp.where(((voxel >> 4) & 1) * 2 + (voxel & 1) == k, 1.0, 0.0)
        parities.append(jnp.broadcast_to(hit, (64, PLANE)).astype(BF16))
    for r in range(2):
        row_key = jnp.where((row >> 6) == r, row & 63, -1)
        spread = mm(pieces, one_hot(row_key, (lane >> 5) * HALF + ((lane >> 1) & 7))).astype(BF16)
        for wz in range(HALF):
            for k in range(4):
                up_ref[r, wz, pl.ds(k * 64, 64), :] = spread[wz * 64 : (wz + 1) * 64] * parities[k]
    side_cols = []
    for (other, dz, z), ref in zip(sides, (core_ref, cross_ref)):
        for r in range(2):
            side_cols.append(unfold_side(xy_ref, layers, layer, r, other, ref[...]))
    for copy in copies[:3]:
        copy.wait()
    small_ref[...] = mask_ref[...].astype(F32).astype(BF16)
    for side, (other, dz, z) in enumerate(sides):
        for r in range(2):
            acc_ref[r, rows_at(15 - z), :] += mm(stacked_ref[rows_at(dz), :], side_cols[side * 2 + r])
    zeros = jnp.zeros((64, PLANE), BF16)
    for r in range(2):
        grad_ref[r, pl.ds(0, 64), :] = zeros
        grad_ref[r, pl.ds(18 * 32, 64), :] = zeros
        for wz in range(HALF):
            grad_act = mm(down_t_ref[...], up_ref[r, wz])
            for kz in range(2):
                z = 2 * wz + kz
                mask = mask_ref[pl.ds(r, 1), pl.ds(z * PLANE, PLANE)].astype(F32)
                pre = acc_ref[r, pl.ds((15 - z) * 32, 32), :]
                sig = 1.0 / (1.0 + jnp.exp(-pre))
                masked = sig * mask
                act_ref[pl.ds(z * 32, 32), pl.ds(r * PLANE, PLANE)] = (pre * masked).astype(BF16)
                grad = grad_act[kz * 32 : (kz + 1) * 32] * masked * (1.0 + pre * (1.0 - sig))
                grad = grad.astype(BF16)
                grad_ref[r, pl.ds((17 - z) * 32, 32), :] = grad
                gplanes_ref[pl.ds(z * 32, 32), pl.ds(r * PLANE, PLANE)] = grad
        for (other, dz, z), ref in zip(sides, (gcore_ref, gcross_ref)):
            ref[:, pl.ds(r * PLANE, PLANE)] = grad_ref[r, rows_at(17 - z), :]

    for ky in range(2):
        found = mm(act_ref[...], gather_ref[ky]).astype(BF16)
        for z in range(EDGE):
            for kx in range(2):
                rows = pl.ds((z % 2) * 128 + (ky * 2 + kx) * 32, 32)
                stride_ref[rows, pl.ds((z // 2) * 128, 128)] = found[z * 32 : (z + 1) * 32, kx * 128 : (kx + 1) * 128]
    oct_ref[...] = mm(down_ref[...], stride_ref[...]).astype(BF16)
    down_sum = mm_nt(grad_oct, stride_ref[...]) * scale
    sums_ref[:, pl.ds(896, 256)] = down_sum[:32]
    sums_ref[:, pl.ds(1152, 256)] = down_sum[32:]

    copies[3].wait()
    total = jnp.zeros((288, 96), F32)
    for r in range(2):
        for p in range(EDGE):
            total += mm_nt(cols_ref[r, pl.ds(p * 288, 288), :], grad_ref[r, pl.ds((EDGE - p) * 32, 96), :])
    total_ref[...] = total.T
    for side, (other, dz, z) in enumerate(sides):
        for r in range(2):
            total_ref[rows_at(dz), :] += mm_nt(grad_ref[r, rows_at(17 - z), :], side_cols[side * 2 + r])
    total = [total_ref[pl.ds(dz * 32, 32), :] for dz in range(3)]
    sums_ref[:, pl.ds(0, 896)] = jnp.concatenate([*total, jnp.zeros((32, 32), F32)], axis=1) * scale


def back_inner_kernel(xy_ref, after_ref, gplanes_ref, flipped_ref, acc_ref, rows_ref, window_ref, cols_ref):
    layer = lax.axis_index("morton")
    build_masks(0, 0, rows_ref, window_ref.at[0])
    for r in range(2):
        ox, oy = offset_of(xy_ref, layer, r, layer, 1 - r)
        build_masks(ox, oy, rows_ref, window_ref.at[1 + r])
        for i in range(2):
            unfold_planes(gplanes_ref, r, i * STEP, ox, window_ref.at[0], window_ref.at[1 + r], cols_ref.at[r])
        convolve(flipped_ref[...], cols_ref.at[r], acc_ref.at[r])


def back_outer_kernel(layers, xy_ref, mask_ref, after_ref, acc_ref, recv_ref, cross_ref, flipped_ref, out_hbm, out_ref, sems):
    core_ref = recv_ref.at[pl.ds(64, 32), pl.ds(0, 2 * PLANE)]
    layer = lax.axis_index("morton")
    odd = layer % 2
    out = []
    for r in range(2):
        terms = []
        for (other, dz, z), ref in zip(sides_of(layer), (core_ref, cross_ref)):
            terms.append(mm(flipped_ref[rows_at(dz), :], unfold_side(xy_ref, layers, layer, r, other, ref[...])))
        below = jnp.where(odd == 1, terms[0], terms[1])
        above = jnp.where(odd == 1, terms[1], terms[0])
        for z in range(EDGE):
            lanes = pl.ds(z * PLANE, PLANE)
            mask = mask_ref[pl.ds(r, 1), lanes].astype(F32)
            grad = acc_ref[r, pl.ds((17 - z) * 32, 32), :]
            if z == 0:
                grad = grad + below
            if z == EDGE - 1:
                grad = grad + above
            out_ref[r, :, lanes] = (grad * mask).astype(BF16)
        out += start_all(((out_ref.at[r], out_hbm.at[r]),), sems.at[pl.ds(r, 1)])
    for copy in out:
        copy.wait()


def finish_kernel(total_ref, other_ref, conv_ref, down_ref):
    odd = lax.axis_index("morton") % 2
    for place, ref in ((odd, total_ref), (1 - odd, other_ref)):
        rows = pl.ds(pl.multiple_of(place * 16, 16), 16)
        conv_ref[rows, :] = ref[:, pl.ds(0, 864)]
        down_ref[rows, :] = ref[:, pl.ds(896, 256)]
        down_ref[pl.ds(pl.multiple_of(place * 16 + 32, 16), 16), :] = ref[:, pl.ds(1152, 256)]


def coarse_kernel(xy_ref, own_ref, recv_ref, after_ref, out_hbm, out_ref, sems):
    layer = lax.axis_index("morton")
    parity = layer % 2
    partner = layer + 1 - 2 * parity
    out = []
    for i, (target, half, ref) in enumerate(((layer, parity, own_ref), (partner, 1 - parity, recv_ref))):
        pieces = jnp.concatenate([ref[:64, wz * 128 : (wz + 1) * 128] for wz in range(HALF)], axis=0)
        key = octant_key(xy_ref, target, parity, iota((128, 128), 0))
        places = [one_hot(key, iota((128, 128), 1) + tile * 128) for tile in range(4)]
        lanes = pl.ds(pl.multiple_of(half * HALF * PLANE, HALF * PLANE), HALF * PLANE)
        for q in range(2):
            placed = mm(pieces, jnp.concatenate(places[2 * q : 2 * q + 2], axis=1)).astype(BF16)
            for wz in range(HALF):
                out_ref[i, q, :, pl.ds(wz * PLANE, PLANE)] = placed[wz * 64 : (wz + 1) * 64]
            out += start_all(((out_ref.at[i, q], out_hbm.at[q, :, lanes]),), sems.at[pl.ds(2 * i + q, 1)])
    for copy in out:
        copy.wait()


def call(body, name, out_shapes, operands, kinds, scratch=(), us=1, out_kinds=None, vmem_mib=24):
    specs = {"s": pl.BlockSpec(memory_space=pltpu.SMEM), "h": pl.BlockSpec(memory_space=pl.ANY)}
    specs["v"] = pl.BlockSpec(memory_space=pltpu.VMEM)
    single = not isinstance(out_shapes, list)
    out_specs = [specs[kind] for kind in out_kinds or "v" * (1 if single else len(out_shapes))]
    return pl.pallas_call(
        body,
        name=name,
        out_shape=out_shapes,
        in_specs=[specs[kind] for kind in kinds],
        out_specs=out_specs[0] if single else out_specs,
        scratch_shapes=list(scratch),
        compiler_params=pltpu.CompilerParams(vmem_limit_bytes=vmem_mib << 20),
        cost_estimate=pl.CostEstimate(flops=us * 10**9, bytes_accessed=us * 3500000, transcendentals=0),
    )(*operands)


def shape(dims, dtype=BF16):
    return jax.ShapeDtypeStruct(dims, dtype)


def exchange(value, bit):
    return lax.ppermute(value, "morton", [(i, i ^ (1 << bit)) for i in range(lax.axis_size("morton"))])


def exchange_cross(value):
    layers = lax.axis_size("morton")
    groups = lax.axis_size("groups")
    pairs = []
    for g in range(groups):
        for i in range(layers):
            other = i + 1 if i % 2 else i - 1
            if 0 <= other < layers:
                pairs.append((g * layers + i, g * layers + other))
            elif g ^ 1 < groups:
                pairs.append((g * layers + i, (g ^ 1) * layers + i))
    return lax.ppermute(value, ("groups", "morton"), pairs)


def per_device(features, voxel_mask, brick_xy, neighbours, conv_weight, down_weight, coarse_grad):
    bricks, channels, voxels = features.shape
    layers = lax.axis_size("morton")
    rounds = layers.bit_length() - 1
    scale = 1.0 / math.sqrt(bricks * layers * voxels)
    side_shape = shape((32, 2 * PLANE))
    oct_shape = shape((64, 1024))
    message_shape = shape((96, 1024))
    xy = brick_xy.T
    pinned = [pltpu.with_memory_space_constraint(x, pltpu.HBM) for x in (xy, features, voxel_mask, coarse_grad, conv_weight, down_weight)]
    block = shape((96, 288))
    message, cross_edge, own, flipped, stacked, down_t = call(
        prepare_kernel, "prepare", [message_shape, side_shape, oct_shape, block, block, shape((64, 256))],
        pinned, "shhhhh",
        scratch=[
            pltpu.VMEM((2, 2, 32, PLANE), BF16), pltpu.VMEM((2, 2, PLANE), I32),
            pltpu.VMEM((2, 2, 64, HALF * PLANE), BF16), pltpu.VMEM((32, 864), BF16), pltpu.VMEM((64, 256), BF16),
            pltpu.SemaphoreType.DMA((8,)),
        ],
        us=2, vmem_mib=32,
    )
    arrived = exchange(message, 0)
    cross_side = exchange_cross(cross_edge)
    two_cols = pltpu.VMEM((2, 16 * 288, PLANE), BF16)
    mask = pltpu.VMEM((2, voxels), I32)
    windows = pltpu.VMEM((3, 9, 32, PLANE), BF16)
    mask_rows = pltpu.VMEM((16, PLANE), F32)
    all_cols, acc = call(
        inner_kernel, "forward_own_planes",
        [shape((2, 16 * 288, PLANE)), shape((2, 4096, PLANE), F32)],
        (xy, features, voxel_mask, stacked), "svvv", out_kinds="hh",
        scratch=[
            mask_rows, windows,
            pltpu.VMEM((512, 512), BF16),
            two_cols, pltpu.VMEM((2, 20 * 32, PLANE), F32), pltpu.SemaphoreType.DMA((6,)),
        ],
        us=5, vmem_mib=50,
    )
    message, gplanes, gcross, small_mask, sums = call(
        functools.partial(outer_kernel, layers, scale), "forward_rest",
        [message_shape, shape((512, 512)), side_shape, shape((2, voxels)), shape((32, 1408), F32)],
        (xy, all_cols, acc, voxel_mask, down_weight, arrived, cross_side, own, stacked, down_t), "shhhhvvvvv",
        scratch=[
            two_cols, pltpu.VMEM((2, 512, PLANE), F32), mask, pltpu.VMEM((64, 256), BF16),
            pltpu.VMEM((2, 512, PLANE), BF16), pltpu.VMEM((512, 512), BF16), pltpu.VMEM((2, HALF, 256, PLANE), BF16), pltpu.VMEM((256, 1024), BF16),
            pltpu.VMEM((2, 20 * 32, PLANE), BF16), pltpu.VMEM((96, 288), F32), pltpu.SemaphoreType.DMA((4,)),
        ],
        us=6, vmem_mib=50,
    )
    odd = lax.axis_index("morton") % 2
    rows = sums.shape[0] // 2
    keep = lax.dynamic_slice_in_dim(sums, odd * rows, rows, 0)
    total = keep + exchange(lax.dynamic_slice_in_dim(sums, (1 - odd) * rows, rows, 0), 0)
    message_there = exchange(message, 0)
    for bit in range(1, rounds):
        if bit < 2:
            sent = total
            step = exchange(sent, bit)
        else:
            sent = lax.reduce_precision(total, 8, 7)
            step = exchange(sent.astype(BF16), bit).astype(F32)
        if bit == 1:
            gcross, _ = lax.optimization_barrier((gcross, total))
            gcross_side = exchange_cross(gcross)
            coarse_out = call(
                coarse_kernel, "place", shape((2, 64, voxels)), (xy, message, message_there, total), "svvh", out_kinds="h",
                scratch=[pltpu.VMEM((2, 2, 64, HALF * PLANE), BF16), pltpu.SemaphoreType.DMA((4,))], us=2,
            )
            step, coarse_out = lax.optimization_barrier((step, coarse_out))
        if bit == 2:
            back = call(
                back_inner_kernel, "backward_own_planes", shape((2, 20 * 32, PLANE), F32),
                (xy, total, gplanes, flipped), "shvv", scratch=[mask_rows, windows, two_cols], us=3,
            )
            step, back = lax.optimization_barrier((step, back))
        if bit == 3:
            input_grad = call(
                functools.partial(back_outer_kernel, layers), "backward_rest", shape((bricks, channels, voxels)),
                (xy, small_mask, total, back, message_there, gcross_side, flipped), "svhvvvv", out_kinds="h",
                scratch=[pltpu.VMEM((bricks, channels, voxels), BF16), pltpu.SemaphoreType.DMA((2,))], us=2,
            )
            step, input_grad = lax.optimization_barrier((step, input_grad))
        total = sent + step
    other = exchange(total, 0)
    conv_grad, down_grad = call(
        finish_kernel, "finish", [shape((32, 864), F32), shape((64, 256), F32)], (total, other), "vv"
    )
    return coarse_out, input_grad, conv_grad, down_grad


def solution(mesh):
    return jax.shard_map(
        per_device,
        mesh=mesh,
        in_specs=(
            P(("groups", "morton"), None, None),
            P(("groups", "morton"), None),
            P("groups", None),
            P(("groups", "morton"), None),
            P(),
            P(),
            P(("groups", "morton"), None, None),
        ),
        out_specs=(
            P(("groups", "morton"), None, None),
            P(("groups", "morton"), None, None),
            P("groups", None),
            P("groups", None),
        ),
        check_vma=False,
    )
```

```python
import functools
import math

import jax
import jax.numpy as jnp
from jax import lax
from jax.experimental import pallas as pl
from jax.experimental.pallas import tpu as pltpu
from jax.sharding import PartitionSpec as P

EDGE = 16
HALF = 8
PLANE = EDGE * EDGE
QUARTER = HALF * HALF
BF16 = jnp.bfloat16
F32 = jnp.float32
I32 = jnp.int32
STEP = 8


def iota(shape, dim):
    return lax.broadcasted_iota(I32, shape, dim)


def one_hot(row_key, column_key):
    return jnp.where(row_key == column_key, 1.0, 0.0).astype(BF16)


def mm(a, b):
    return jnp.dot(a, b, preferred_element_type=F32)


def mm_nt(a, b):
    return lax.dot_general(a, b, (((1,), (1,)), ((), ())), preferred_element_type=F32)


def xy_of(xy_ref, layer, brick):
    return xy_ref[0, layer * 2 + brick], xy_ref[1, layer * 2 + brick]


def octant_key(xy_ref, layer, parity, lane):
    brick = (lane >> 6) & 1
    bases = []
    for b in range(2):
        x, y = xy_of(xy_ref, layer, b)
        base = (x // 2) * PLANE + (y % 2) * HALF * EDGE + (x % 2) * HALF
        bases.append(jnp.where(y // 2 == parity, base, -65536))
    return jnp.where(brick == 0, bases[0], bases[1]) + ((lane >> 3) & 7) * EDGE + (lane & 7)


def start_all(pairs, sems):
    copies = [pltpu.make_async_copy(source, target, sems.at[i]) for i, (source, target) in enumerate(pairs)]
    for copy in copies:
        copy.start()
    return copies


def prepare_kernel(
    xy_ref, feat_hbm, mask_hbm, grad_hbm, weight_hbm, down_hbm,
    send_ref, cross_ref, own_ref, flipped_ref, stacked_ref, down_t_ref,
    feat_ref, mask_ref, grad_ref, weight_ref, down_ref, sems,
):
    layer = lax.axis_index("morton")
    parity = layer % 2
    partner = layer + 1 - 2 * parity
    halves = [
        grad_hbm.at[:, :, pl.ds(pl.multiple_of(half * HALF * PLANE, HALF * PLANE), HALF * PLANE)]
        for half in (1 - parity, parity)
    ]
    pairs = [(weight_hbm, weight_ref), (down_hbm, down_ref)]
    for side in range(2):
        z = jnp.where(parity == side, EDGE - 1, 0)
        lanes = pl.ds(pl.multiple_of(z * PLANE, PLANE), PLANE)
        pairs += [(feat_hbm.at[:, :, lanes], feat_ref.at[side]), (mask_hbm.at[:, lanes], mask_ref.at[side])]
    pairs += [(halves[0], grad_ref.at[0]), (halves[1], grad_ref.at[1])]
    copies = start_all(pairs, sems)
    row = iota((2 * PLANE, 2 * QUARTER), 0)
    lane = iota((1, 2 * QUARTER), 1)
    picks = [one_hot(row, octant_key(xy_ref, target, parity, lane)) for target in (partner, layer)]
    for copy in copies[:2]:
        copy.wait()
    flipped = weight_ref[...].astype(F32).T.astype(BF16)
    for dz in range(3):
        rows = pl.ds(dz * 32, 32)
        blocks = [flipped[j * 32 : (j + 1) * 32] for j in (26 - dz * 9 - s for s in range(9))]
        flipped_ref[rows, :] = jnp.concatenate(blocks, axis=1)
        stacked_ref[rows, :] = weight_ref[:, pl.ds(dz * 288, 288)]
    down_t = down_ref[...].astype(F32).T.astype(BF16)
    for kz in range(2):
        blocks = [down_t[(kz * 4 + k) * 32 : (kz * 4 + k + 1) * 32] for k in range(4)]
        down_t_ref[pl.ds(kz * 32, 32), :] = jnp.concatenate(blocks, axis=1)
    for copy in copies[2:6]:
        copy.wait()
    for side, ref in enumerate((send_ref.at[pl.ds(64, 32)], cross_ref)):
        for r in range(2):
            mask = mask_ref[side, pl.ds(r, 1), :].astype(F32).astype(BF16)
            ref[:, pl.ds(r * PLANE, PLANE)] = feat_ref[side, r] * mask
    for i, ref in enumerate((send_ref.at[pl.ds(0, 64)], own_ref)):
        copies[6 + i].wait()
        planes = [
            jnp.concatenate([grad_ref[i, q, :, pl.ds(wz * PLANE, PLANE)] for q in range(2)], axis=1) for wz in range(HALF)
        ]
        found = mm(jnp.concatenate(planes, axis=0), picks[i]).astype(BF16)
        for wz in range(HALF):
            ref[:, pl.ds(wz * 2 * QUARTER, 2 * QUARTER)] = found[wz * 64 : (wz + 1) * 64]


def window_mask(shift, ox, oy):
    dy, dx = shift // 3 - 1, shift % 3 - 1
    voxel = (iota((1, PLANE), 1) - (EDGE * dy + dx)) & (PLANE - 1)
    x = (voxel & (EDGE - 1)) + dx - EDGE * ox
    y = (voxel >> 4) + dy - EDGE * oy
    inside = jnp.where(((x | y) & -EDGE) == 0, 1.0, 0.0)
    return jnp.broadcast_to(inside, (32, PLANE)).astype(BF16)


def offset_of(xy_ref, layer, r, other, s):
    x, y = xy_of(xy_ref, layer, r)
    near_x, near_y = xy_of(xy_ref, other, s)
    return near_x - x, near_y - y


def turned(planes, ox):
    return pltpu.roll(planes, (ox * EDGE) & (PLANE - 1), 1)


def shifted(first, second, masks, shift):
    dy, dx = shift // 3 - 1, shift % 3 - 1
    times = first.shape[0] // 32
    both = first * jnp.tile(masks[0], (times, 1)) + second * jnp.tile(masks[1], (times, 1))
    back = (-(EDGE * dy + dx)) & (PLANE - 1)
    return pltpu.roll(both, back, 1) if back else both


def build_masks(ox, oy, rows_ref, mask_ref):
    shift = iota((16, PLANE), 0)
    dy = (shift >= 3).astype(I32) + (shift >= 6).astype(I32) - 1
    dx = shift - 3 * dy - 4
    voxel = (iota((16, PLANE), 1) - (EDGE * dy + dx)) & (PLANE - 1)
    x = (voxel & (EDGE - 1)) + dx - EDGE * ox
    y = (voxel >> 4) + dy - EDGE * oy
    rows_ref[...] = jnp.where(((x | y) & -EDGE) == 0, 1.0, 0.0)
    for s in range(9):
        mask_ref[s] = jnp.broadcast_to(rows_ref[pl.ds(s, 1), :], (32, PLANE)).astype(BF16)


def unfold_planes(planes_ref, r, first, ox, own_ref, other_ref, cols_ref):
    for p in range(first, first + STEP, STEP):
        rows = pl.ds(p * 32, STEP * 32)
        own = planes_ref[rows, pl.ds(r * PLANE, PLANE)]
        other = turned(planes_ref[rows, pl.ds((1 - r) * PLANE, PLANE)], ox)
        for shift in range(9):
            piece = own if shift == 4 else shifted(own, other, (own_ref[shift], other_ref[shift]), shift)
            for q in range(STEP):
                cols_ref[pl.ds((p + q) * 288 + shift * 32, 32), :] = piece[q * 32 : (q + 1) * 32]


def unfold_side(xy_ref, layers, layer, r, other, planes):
    valid = (other >= 0) & (other < layers)
    near = jnp.clip(other, 0, layers - 1)
    places = [offset_of(xy_ref, layer, r, near, s) for s in range(2)]
    places = [(jnp.where(valid, ox, 8), oy) for ox, oy in places]
    first, second = (turned(planes[:, s * PLANE : (s + 1) * PLANE], places[s][0]) for s in range(2))
    pieces = []
    for shift in range(9):
        masks = [window_mask(shift, ox, oy) for ox, oy in places]
        pieces.append(shifted(first, second, masks, shift))
    return jnp.concatenate(pieces, axis=0)


def convolve(stacked, cols_ref, acc_ref):
    acc_ref[...] = jnp.zeros(acc_ref.shape, F32)
    for p in range(EDGE):
        rows = pl.ds((EDGE - p) * 32, 96)
        acc_ref[rows, :] += mm(stacked, cols_ref[pl.ds(p * 288, 288), :])


def inner_kernel(
    xy_ref, feat_ref, mask_ref, stacked_ref, cols_hbm, acc_ref, rows_ref, window_ref, in_ref, cols_ref, sems,
):
    layer = lax.axis_index("morton")
    build_masks(0, 0, rows_ref, window_ref.at[2])
    ox = []
    for r in range(2):
        x, y = offset_of(xy_ref, layer, r, layer, 1 - r)
        build_masks(x, y, rows_ref, window_ref.at[r])
        ox.append(x)
    for r in range(2):
        for z in range(EDGE):
            lanes = pl.ds(z * PLANE, PLANE)
            mask = mask_ref[pl.ds(r, 1), lanes].astype(F32).astype(BF16)
            in_ref[pl.ds(z * 32, 32), pl.ds(r * PLANE, PLANE)] = feat_ref[r, :, lanes] * mask
    out = []
    for r in range(2):
        for i in range(2):
            unfold_planes(in_ref, r, i * STEP, ox[r], window_ref.at[2], window_ref.at[r], cols_ref.at[r])
            rows = pl.ds(i * STEP * 288, STEP * 288)
            out += start_all(((cols_ref.at[r, rows], cols_hbm.at[r, rows]),), sems.at[pl.ds(2 * r + i, 1)])
    for r in range(2):
        convolve(stacked_ref[...], cols_ref.at[r], acc_ref.at[r])
    for copy in out:
        copy.wait()


def sides_of(layer):
    odd = layer % 2
    core = jnp.where(odd == 0, layer + 1, layer - 1)
    cross = jnp.where(odd == 0, layer - 1, layer + 1)
    return ((core, 2 * (1 - odd), 15 * (1 - odd)), (cross, 2 * odd, 15 * odd))


def rows_at(index):
    return pl.ds(pl.multiple_of(index * 32, 32), 32)


def outer_kernel(
    layers, scale, xy_ref, cols_hbm, acc_ref, mask_hbm, down_hbm, recv_ref, cross_ref, own_ref, stacked_ref, down_t_ref,
    message_ref, gplanes_ref, gcross_ref, small_ref, sums_ref,
    cols_ref, side_ref, mask_ref, down_ref, gather_ref, act_ref, up_ref, stride_ref, grad_ref, total_ref, sems,
):
    copies = start_all(
        ((mask_hbm, mask_ref), (down_hbm, down_ref), (cols_hbm, cols_ref)), sems
    )
    layer = lax.axis_index("morton")
    sides = sides_of(layer)

    row = iota((2 * PLANE, PLANE), 0)
    lane = iota((2 * PLANE, PLANE), 1)
    row_key = (row >> 8) * 4096 + ((row >> 4) & 15) * 64 + (row & 15)
    lane_key = ((lane >> 6) & 1) * 4096 + ((lane >> 3) & 7) * 128 + (lane & 7) * 2 + (lane >> 7)
    for ky in range(2):
        gather_ref[ky] = one_hot(row_key, lane_key + ky * 64)

    core_ref = recv_ref.at[pl.ds(64, 32), pl.ds(0, 2 * PLANE)]
    oct_ref = message_ref.at[pl.ds(0, 64)]
    gcore_ref = message_ref.at[pl.ds(64, 32), pl.ds(0, 2 * PLANE)]
    grad_oct = own_ref[...] + recv_ref[pl.ds(0, 64), :]
    pieces = jnp.concatenate([grad_oct[:, wz * 128 : (wz + 1) * 128] for wz in range(HALF)], axis=0)
    row = iota((128, PLANE), 0)
    lane = iota((128, PLANE), 1)
    parities = []
    for k in range(4):
        voxel = iota((1, PLANE), 1)
        hit = jnp.where(((voxel >> 4) & 1) * 2 + (voxel & 1) == k, 1.0, 0.0)
        parities.append(jnp.broadcast_to(hit, (64, PLANE)).astype(BF16))
    for r in range(2):
        row_key = jnp.where((row >> 6) == r, row & 63, -1)
        spread = mm(pieces, one_hot(row_key, (lane >> 5) * HALF + ((lane >> 1) & 7))).astype(BF16)
        for wz in range(HALF):
            for k in range(4):
                up_ref[r, wz, pl.ds(k * 64, 64), :] = spread[wz * 64 : (wz + 1) * 64] * parities[k]
    side_cols = []
    for (other, dz, z), ref in zip(sides, (core_ref, cross_ref)):
        for r in range(2):
            side_cols.append(unfold_side(xy_ref, layers, layer, r, other, ref[...]))
    for copy in copies[:2]:
        copy.wait()
    small_ref[...] = mask_ref[...].astype(F32).astype(BF16)
    for side, (other, dz, z) in enumerate(sides):
        for r in range(2):
            side_ref[r, dz // 2] = mm(stacked_ref[rows_at(dz), :], side_cols[side * 2 + r])
    zeros = jnp.zeros((64, PLANE), BF16)
    for r in range(2):
        grad_ref[r, pl.ds(0, 64), :] = zeros
        grad_ref[r, pl.ds(18 * 32, 64), :] = zeros
        for wz in range(HALF):
            grad_act = mm(down_t_ref[...], up_ref[r, wz])
            for kz in range(2):
                z = 2 * wz + kz
                mask = mask_ref[pl.ds(r, 1), pl.ds(z * PLANE, PLANE)].astype(F32)
                pre = acc_ref[r, pl.ds((17 - z) * 32, 32), :]
                if z in (0, EDGE - 1):
                    pre = pre + side_ref[r, z // (EDGE - 1)]
                sig = 1.0 / (1.0 + jnp.exp(-pre))
                masked = sig * mask
                act_ref[pl.ds(z * 32, 32), pl.ds(r * PLANE, PLANE)] = (pre * masked).astype(BF16)
                grad = grad_act[kz * 32 : (kz + 1) * 32] * masked * (1.0 + pre * (1.0 - sig))
                grad = grad.astype(BF16)
                grad_ref[r, pl.ds((17 - z) * 32, 32), :] = grad
                gplanes_ref[pl.ds(z * 32, 32), pl.ds(r * PLANE, PLANE)] = grad
        for (other, dz, z), ref in zip(sides, (gcore_ref, gcross_ref)):
            ref[:, pl.ds(r * PLANE, PLANE)] = grad_ref[r, rows_at(17 - z), :]

    for ky in range(2):
        found = mm(act_ref[...], gather_ref[ky]).astype(BF16)
        for z in range(EDGE):
            for kx in range(2):
                rows = pl.ds((z % 2) * 128 + (ky * 2 + kx) * 32, 32)
                stride_ref[rows, pl.ds((z // 2) * 128, 128)] = found[z * 32 : (z + 1) * 32, kx * 128 : (kx + 1) * 128]
    oct_ref[...] = mm(down_ref[...], stride_ref[...]).astype(BF16)
    down_sum = mm_nt(grad_oct, stride_ref[...]) * scale
    sums_ref[:, pl.ds(896, 256)] = down_sum[:32]
    sums_ref[:, pl.ds(1152, 256)] = down_sum[32:]

    copies[2].wait()
    total = jnp.zeros((288, 96), F32)
    for r in range(2):
        for p in range(EDGE):
            total += mm_nt(cols_ref[r, pl.ds(p * 288, 288), :], grad_ref[r, pl.ds((EDGE - p) * 32, 96), :])
    total_ref[...] = total.T
    for side, (other, dz, z) in enumerate(sides):
        for r in range(2):
            total_ref[rows_at(dz), :] += mm_nt(grad_ref[r, rows_at(17 - z), :], side_cols[side * 2 + r])
    total = [total_ref[pl.ds(dz * 32, 32), :] for dz in range(3)]
    sums_ref[:, pl.ds(0, 896)] = jnp.concatenate([*total, jnp.zeros((32, 32), F32)], axis=1) * scale


def back_inner_kernel(xy_ref, after_ref, gplanes_ref, flipped_ref, acc_ref, rows_ref, window_ref, cols_ref):
    layer = lax.axis_index("morton")
    build_masks(0, 0, rows_ref, window_ref.at[0])
    for r in range(2):
        ox, oy = offset_of(xy_ref, layer, r, layer, 1 - r)
        build_masks(ox, oy, rows_ref, window_ref.at[1 + r])
        for i in range(2):
            unfold_planes(gplanes_ref, r, i * STEP, ox, window_ref.at[0], window_ref.at[1 + r], cols_ref.at[r])
        convolve(flipped_ref[...], cols_ref.at[r], acc_ref.at[r])


def back_outer_kernel(layers, xy_ref, mask_ref, after_ref, acc_ref, recv_ref, cross_ref, flipped_ref, out_hbm, out_ref, sems):
    core_ref = recv_ref.at[pl.ds(64, 32), pl.ds(0, 2 * PLANE)]
    layer = lax.axis_index("morton")
    odd = layer % 2
    out = []
    for r in range(2):
        terms = []
        for (other, dz, z), ref in zip(sides_of(layer), (core_ref, cross_ref)):
            terms.append(mm(flipped_ref[rows_at(dz), :], unfold_side(xy_ref, layers, layer, r, other, ref[...])))
        below = jnp.where(odd == 1, terms[0], terms[1])
        above = jnp.where(odd == 1, terms[1], terms[0])
        for z in range(EDGE):
            lanes = pl.ds(z * PLANE, PLANE)
            mask = mask_ref[pl.ds(r, 1), lanes].astype(F32)
            grad = acc_ref[r, pl.ds((17 - z) * 32, 32), :]
            if z == 0:
                grad = grad + below
            if z == EDGE - 1:
                grad = grad + above
            out_ref[r, :, lanes] = (grad * mask).astype(BF16)
        out += start_all(((out_ref.at[r], out_hbm.at[r]),), sems.at[pl.ds(r, 1)])
    for copy in out:
        copy.wait()


def finish_kernel(total_ref, other_ref, conv_ref, down_ref):
    odd = lax.axis_index("morton") % 2
    for place, ref in ((odd, total_ref), (1 - odd, other_ref)):
        rows = pl.ds(pl.multiple_of(place * 16, 16), 16)
        conv_ref[rows, :] = ref[:, pl.ds(0, 864)]
        down_ref[rows, :] = ref[:, pl.ds(896, 256)]
        down_ref[pl.ds(pl.multiple_of(place * 16 + 32, 16), 16), :] = ref[:, pl.ds(1152, 256)]


def coarse_kernel(xy_ref, own_ref, recv_ref, after_ref, out_hbm, out_ref, sems):
    layer = lax.axis_index("morton")
    parity = layer % 2
    partner = layer + 1 - 2 * parity
    out = []
    for i, (target, half, ref) in enumerate(((layer, parity, own_ref), (partner, 1 - parity, recv_ref))):
        pieces = jnp.concatenate([ref[:64, wz * 128 : (wz + 1) * 128] for wz in range(HALF)], axis=0)
        key = octant_key(xy_ref, target, parity, iota((128, 128), 0))
        places = [one_hot(key, iota((128, 128), 1) + tile * 128) for tile in range(4)]
        lanes = pl.ds(pl.multiple_of(half * HALF * PLANE, HALF * PLANE), HALF * PLANE)
        for q in range(2):
            placed = mm(pieces, jnp.concatenate(places[2 * q : 2 * q + 2], axis=1)).astype(BF16)
            for wz in range(HALF):
                out_ref[i, q, :, pl.ds(wz * PLANE, PLANE)] = placed[wz * 64 : (wz + 1) * 64]
            out += start_all(((out_ref.at[i, q], out_hbm.at[q, :, lanes]),), sems.at[pl.ds(2 * i + q, 1)])
    for copy in out:
        copy.wait()


def call(body, name, out_shapes, operands, kinds, scratch=(), us=1, out_kinds=None, vmem_mib=24):
    specs = {"s": pl.BlockSpec(memory_space=pltpu.SMEM), "h": pl.BlockSpec(memory_space=pl.ANY)}
    specs["v"] = pl.BlockSpec(memory_space=pltpu.VMEM)
    single = not isinstance(out_shapes, list)
    out_specs = [specs[kind] for kind in out_kinds or "v" * (1 if single else len(out_shapes))]
    return pl.pallas_call(
        body,
        name=name,
        out_shape=out_shapes,
        in_specs=[specs[kind] for kind in kinds],
        out_specs=out_specs[0] if single else out_specs,
        scratch_shapes=list(scratch),
        compiler_params=pltpu.CompilerParams(vmem_limit_bytes=vmem_mib << 20),
        cost_estimate=pl.CostEstimate(flops=us * 10**9, bytes_accessed=us * 3500000, transcendentals=0),
    )(*operands)


def shape(dims, dtype=BF16):
    return jax.ShapeDtypeStruct(dims, dtype)


def exchange(value, bit):
    return lax.ppermute(value, "morton", [(i, i ^ (1 << bit)) for i in range(lax.axis_size("morton"))])


def exchange_cross(value):
    layers = lax.axis_size("morton")
    groups = lax.axis_size("groups")
    pairs = []
    for g in range(groups):
        for i in range(layers):
            other = i + 1 if i % 2 else i - 1
            if 0 <= other < layers:
                pairs.append((g * layers + i, g * layers + other))
            elif g ^ 1 < groups:
                pairs.append((g * layers + i, (g ^ 1) * layers + i))
    return lax.ppermute(value, ("groups", "morton"), pairs)


def per_device(features, voxel_mask, brick_xy, neighbours, conv_weight, down_weight, coarse_grad):
    bricks, channels, voxels = features.shape
    layers = lax.axis_size("morton")
    rounds = layers.bit_length() - 1
    scale = 1.0 / math.sqrt(bricks * layers * voxels)
    side_shape = shape((32, 2 * PLANE))
    oct_shape = shape((64, 1024))
    message_shape = shape((96, 1024))
    xy = brick_xy.T
    pinned = [pltpu.with_memory_space_constraint(x, pltpu.HBM) for x in (xy, features, voxel_mask, coarse_grad, conv_weight, down_weight)]
    block = shape((96, 288))
    message, cross_edge, own, flipped, stacked, down_t = call(
        prepare_kernel, "prepare", [message_shape, side_shape, oct_shape, block, block, shape((64, 256))],
        pinned, "shhhhh",
        scratch=[
            pltpu.VMEM((2, 2, 32, PLANE), BF16), pltpu.VMEM((2, 2, PLANE), I32),
            pltpu.VMEM((2, 2, 64, HALF * PLANE), BF16), pltpu.VMEM((32, 864), BF16), pltpu.VMEM((64, 256), BF16),
            pltpu.SemaphoreType.DMA((8,)),
        ],
        us=2, vmem_mib=32,
    )
    arrived = exchange(message, 0)
    cross_side = exchange_cross(cross_edge)
    two_cols = pltpu.VMEM((2, 16 * 288, PLANE), BF16)
    mask = pltpu.VMEM((2, voxels), I32)
    windows = pltpu.VMEM((3, 9, 32, PLANE), BF16)
    mask_rows = pltpu.VMEM((16, PLANE), F32)
    all_cols, acc = call(
        inner_kernel, "forward_own_planes",
        [shape((2, 16 * 288, PLANE)), shape((2, 20 * 32, PLANE), F32)],
        (xy, features, voxel_mask, stacked), "svvv", out_kinds="hv",
        scratch=[
            mask_rows, windows,
            pltpu.VMEM((512, 512), BF16),
            two_cols, pltpu.SemaphoreType.DMA((4,)),
        ],
        us=5, vmem_mib=50,
    )
    message, gplanes, gcross, small_mask, sums = call(
        functools.partial(outer_kernel, layers, scale), "forward_rest",
        [message_shape, shape((512, 512)), side_shape, shape((2, voxels)), shape((32, 1408), F32)],
        (xy, all_cols, acc, voxel_mask, down_weight, arrived, cross_side, own, stacked, down_t), "shvhhvvvvv",
        scratch=[
            two_cols, pltpu.VMEM((2, 2, 32, PLANE), F32), mask, pltpu.VMEM((64, 256), BF16),
            pltpu.VMEM((2, 512, PLANE), BF16), pltpu.VMEM((512, 512), BF16), pltpu.VMEM((2, HALF, 256, PLANE), BF16), pltpu.VMEM((256, 1024), BF16),
            pltpu.VMEM((2, 20 * 32, PLANE), BF16), pltpu.VMEM((96, 288), F32), pltpu.SemaphoreType.DMA((3,)),
        ],
        us=6, vmem_mib=50,
    )
    odd = lax.axis_index("morton") % 2
    rows = sums.shape[0] // 2
    keep = lax.dynamic_slice_in_dim(sums, odd * rows, rows, 0)
    total = keep + exchange(lax.dynamic_slice_in_dim(sums, (1 - odd) * rows, rows, 0), 0)
    message_there = exchange(message, 0)
    for bit in range(1, rounds):
        if bit < 3:
            sent = total
            step = exchange(sent, bit)
        else:
            sent = lax.reduce_precision(total, 8, 7)
            step = exchange(sent.astype(BF16), bit).astype(F32)
        if bit == 1:
            gcross, _ = lax.optimization_barrier((gcross, total))
            gcross_side = exchange_cross(gcross)
            coarse_out = call(
                coarse_kernel, "place", shape((2, 64, voxels)), (xy, message, message_there, total), "svvh", out_kinds="h",
                scratch=[pltpu.VMEM((2, 2, 64, HALF * PLANE), BF16), pltpu.SemaphoreType.DMA((4,))], us=2,
            )
            step, coarse_out = lax.optimization_barrier((step, coarse_out))
        if bit == 2:
            back = call(
                back_inner_kernel, "backward_own_planes", shape((2, 20 * 32, PLANE), F32),
                (xy, total, gplanes, flipped), "shvv", scratch=[mask_rows, windows, two_cols], us=3,
            )
            step, back = lax.optimization_barrier((step, back))
        if bit == 3:
            input_grad = call(
                functools.partial(back_outer_kernel, layers), "backward_rest", shape((bricks, channels, voxels)),
                (xy, small_mask, total, back, message_there, gcross_side, flipped), "svhvvvv", out_kinds="h",
                scratch=[pltpu.VMEM((bricks, channels, voxels), BF16), pltpu.SemaphoreType.DMA((2,))], us=2,
            )
            step, input_grad = lax.optimization_barrier((step, input_grad))
        total = sent + step
    other = exchange(total, 0)
    conv_grad, down_grad = call(
        finish_kernel, "finish", [shape((32, 864), F32), shape((64, 256), F32)], (total, other), "vv"
    )
    return coarse_out, input_grad, conv_grad, down_grad


def solution(mesh):
    return jax.shard_map(
        per_device,
        mesh=mesh,
        in_specs=(
            P(("groups", "morton"), None, None),
            P(("groups", "morton"), None),
            P("groups", None),
            P(("groups", "morton"), None),
            P(),
            P(),
            P(("groups", "morton"), None, None),
        ),
        out_specs=(
            P(("groups", "morton"), None, None),
            P(("groups", "morton"), None, None),
            P("groups", None),
            P("groups", None),
        ),
        check_vma=False,
    )
```
